512 devices in a mesh: tm: 32 (over x, z_lo), dp: 16 (over y, z_hi, core).
Axes of the slice: x: 4, y: 4, z: 16 (z_hi: 2, z_lo: 8; z = z_hi * 8 + z_lo), core: 2. Of those that a mesh axis runs over, the one named last changes fastest.
Arguments:
- video_tokens: float32 [16, 32, 256, 512], P('dp', 'tm'), may hold values from -24 to 24
- actions: int32 [16, 32], P('dp', 'tm'), may hold values from 0 to 127
- frame_times: int32 [16, 32], P('dp'), may hold values from 0 to 93, as said below
- act_table: float32 [128, 512], replicated, may hold values from -3 to 3
- norm_gain: float32 [512], replicated, may hold values from 0.5 to 1.5
- w_qkv: float32 [512, 1536], P('dp'), may hold values from -12 to 12
- w_out: float32 [512, 512], P('dp'), may hold values from -0.25 to 0.25
- slopes: float32 [8], replicated, may hold values from 0.02 to 1
- out_grad: float32 [16, 32, 256, 512], P('dp', 'tm'), may hold values from -6 to 6
Outputs:
- grad_tokens: float32 [16, 32, 256, 512], P('dp', 'tm')
- grad_qkv: float32 [512, 1536], P('dp')
- grad_out: float32 [512, 512], P('dp')
- grad_table: float32 [128, 512], replicated
- grad_gain: float32 [512], replicated
The draws below stay inside these ranges and needn't reach their ends.
Inputs may be any that keep to these rules, and one draw needn't show every extreme that they name: `frame_times`: along each clip's 32 frames the times start at 0 and rise by 1 to 3 from one frame to the next; in some clip every rise is 3.
All inputs are finite; a program needn't handle non-finite values.
Results may differ from the reference program's by a relative error of at most 0.0003.
Values sent between devices are 32-bit elements; how exact they have to be, the bound alone decides.
No kernel may reach another device: no remote copies, remote signals or barrier semaphores. Data moves between devices by JAX's collectives and lax.ppermute only.
A program may use at most 64 MiB of HBM per device.

```python
import math
import jax
import jax.numpy as jnp
from jax import lax

D = 512
HEADS = 8
ACTIONS = 128
PATCHES = 256
FRAMES = 32
CLIPS = 16


def draw_video_tokens(key, part):
    key = jax.random.fold_in(key, 11)
    key_base = jax.random.fold_in(key, 0)
    full_shape = (CLIPS, FRAMES, PATCHES, D)
    return jnp.clip(jax.random.normal(key_base, full_shape, jnp.float32), -6.0, 6.0)


def draw_frame_times(key, part):
    key = jax.random.fold_in(key, 37)
    key_rises, key_chosen = jax.random.split(key)
    rises = jax.random.randint(key_rises, (CLIPS, FRAMES - 1), 1, 4).astype(jnp.int32)
    chosen = jax.random.randint(key_chosen, (), 0, CLIPS).astype(jnp.int32)
    clip_ids = jnp.arange(CLIPS, dtype=jnp.int32)[:, None]
    rises = jnp.where(clip_ids == chosen, jnp.int32(3), rises)
    starts = jnp.zeros((CLIPS, 1), jnp.int32)
    return jnp.concatenate([starts, jnp.cumsum(rises, axis=1).astype(jnp.int32)], axis=1).astype(jnp.int32)


def draw_w_qkv(key, part):
    key = jax.random.fold_in(key, 23)
    key_query = jax.random.fold_in(key, 0)
    spread = D ** (-0.5)
    return jnp.clip(jax.random.normal(key_query, (D, 3 * D), jnp.float32), -6.0, 6.0) * spread


def place_ends(array, stream_key, low, largest):
    extent = array.shape
    place = [jax.random.randint(jax.random.fold_in(stream_key, axis), (), 0, extent[axis]) for axis in range(len(extent))]
    array = array.at[tuple(place)].set(low)
    longest = extent.index(max(extent))
    place[longest] = (place[longest] + 1) % extent[longest]
    return array.at[tuple(place)].set(largest)


def block_scale(stream_key, extent, cuts, smallest, top_value):
    loudness = 1.0
    for position, blocks in cuts:
        draws = jax.random.uniform(jax.random.fold_in(jax.random.fold_in(stream_key, 6), position), (blocks,), jnp.float32, smallest / len(cuts), top_value / len(cuts))
        loudness = loudness * jnp.repeat(jnp.exp(draws), extent[position] // blocks).reshape((-1,) + (1,) * (len(extent) - 1 - position))
    return loudness


def normal_values(stream_key, dims, scale, most, shards=(), kind=jnp.bfloat16):
    factor_of = block_scale(stream_key, dims, shards, -0.22, 0.18) if shards else 1.0
    entries = jax.random.normal(stream_key, dims, jnp.float32) * scale * factor_of
    return jnp.minimum(jnp.maximum(entries, -most), most).astype(kind)


def setup_inputs(seed: int = 0) -> dict:
    keys = jax.random.split(jax.random.key(seed), 10)
    return {
        "video_tokens": draw_video_tokens(jax.random.fold_in(keys[9], 71), 0),
        "actions": place_ends(jax.random.randint(keys[1], (CLIPS, FRAMES), 0, ACTIONS), jax.random.fold_in(keys[1], 1), 0, ACTIONS - 1).astype(jnp.int32),
        "frame_times": draw_frame_times(jax.random.fold_in(keys[9], 71), 0),
        "act_table": normal_values(keys[3], (ACTIONS, D), 0.5, 3.0, (), jnp.float32),
        "norm_gain": jnp.clip(1.0 + 0.1 * jax.random.normal(keys[4], (D,), jnp.float32), 0.5, 1.5),
        "w_qkv": draw_w_qkv(jax.random.fold_in(keys[9], 71), 0),
        "w_out": normal_values(keys[6], (D, D), D ** -0.5, 0.25, ((0, 16),), jnp.float32),
        "slopes": jnp.clip(jnp.exp(jax.random.uniform(keys[7], (HEADS,), jnp.float32, math.log(0.02), math.log(1.0))), 0.02, 1.0),
        "out_grad": normal_values(keys[8], (CLIPS, FRAMES, PATCHES, D), 1.0, 6.0, ((0, 16), (1, 32)), jnp.float32),
    }


precise = lax.Precision.HIGHEST

def attend(qkv_rows, frame_times, slopes, head_count):
    clip_count, frames, patches, triple = qkv_rows.shape
    features = triple // 3
    head_size = features // head_count
    pieces = qkv_rows.reshape(clip_count, frames, patches, 3, head_count, head_size)
    scores = jnp.einsum('cipnd,cjpnd->cpnij', pieces[:, :, :, 0], pieces[:, :, :, 1], precision=precise) / math.sqrt(head_size)
    spacing = (frame_times[:, :, None] - frame_times[:, None, :]).astype(jnp.float32)
    scores = scores - slopes[None, None, :, None, None] * spacing[:, None, None, :, :]
    causal = lax.broadcasted_iota(jnp.int32, (frames, frames), 0) >= lax.broadcasted_iota(jnp.int32, (frames, frames), 1)
    scores = jnp.where(causal, scores, -jnp.inf)
    row_peak = lax.stop_gradient(lax.optimization_barrier(jnp.max(scores, axis=-1, keepdims=True)))
    raised = jnp.exp(scores - row_peak)
    weights = raised / lax.optimization_barrier(jnp.sum(raised, axis=-1, keepdims=True))
    mixed_rows = jnp.einsum('cpnij,cjpnd->cipnd', weights, pieces[:, :, :, 2], precision=precise)
    return mixed_rows.reshape(clip_count, frames, patches, features)

def rms_scale(embedded, norm_gain):
    return embedded * norm_gain * lax.rsqrt(lax.optimization_barrier(jnp.mean(embedded * embedded, axis=-1, keepdims=True)) + 1e-06)

def project(token_rows, matrix):
    return jnp.einsum('cfpd,de->cfpe', token_rows, matrix, precision=precise)

def forward(video_tokens, act_table, norm_gain, w_qkv, w_out, actions, frame_times, slopes):
    lookup = (actions[..., None] == lax.iota(jnp.int32, ACTIONS)).astype(jnp.float32)
    embedded = video_tokens + jnp.einsum('cfa,ad->cfd', lookup, act_table, precision=precise)[:, :, None, :]
    normed = rms_scale(embedded, norm_gain)
    mixed_rows = attend(project(normed, w_qkv), frame_times, slopes, HEADS)
    return embedded + project(mixed_rows, w_out)

def reference(video_tokens, actions, frame_times, act_table, norm_gain, w_qkv, w_out, slopes, out_grad):

    def sublayer(tokens, table, gain, first_matrix, second_matrix):
        return forward(tokens, table, gain, first_matrix, second_matrix, actions, frame_times, slopes)
    _, pullback = jax.vjp(sublayer, video_tokens, act_table, norm_gain, w_qkv, w_out)
    grad_tokens, grad_table, grad_gain, grad_qkv, grad_out = pullback(out_grad)
    return (grad_tokens, grad_qkv, grad_out, grad_table, grad_gain)
```

```python
import functools

import jax
import jax.numpy as jnp
from jax import lax
from jax.experimental import pallas as pl
from jax.experimental.pallas import tpu as pltpu
from jax.sharding import PartitionSpec as P

NX, NZL, NY, NZH, NC = 4, 8, 4, 2, 2
D, QKV, HEADS, HEAD, FRAMES, OWN = 512, 1536, 8, 64, 32, 8
ROWS = FRAMES * OWN
HALF = ROWS // 2
PAIR = 2 * HEAD
ACTIONS = 128
TILES = 35
f32, bf16 = jnp.float32, jnp.bfloat16
BOTH = ("tm", "dp")


def tm_of(x, zl):
    return x * NZL + zl


def dp_of(y, zh, c):
    return (y * NZH + zh) * NC + c


def flat_of(x, zl, y, zh, c):
    return tm_of(x, zl) * (NY * NZH * NC) + dp_of(y, zh, c)


XS, ZLS, YS, ZHS, CS = range(NX), range(NZL), range(NY), range(NZH), range(NC)
X_GROUPS = [[tm_of(x, zl) for x in XS] for zl in ZLS]
ZL_GROUPS = [[tm_of(x, zl) for zl in ZLS] for x in XS]
XY_GROUPS = [
    [flat_of(x, zl, y, zh, c) for x in XS for y in YS] for zl in ZLS for zh in ZHS for c in CS
]
Z_GROUPS = [
    [flat_of(x, zl, y, zh, c) for zh in ZHS for zl in ZLS] for x in XS for y in YS for c in CS
]
SWAP_CORE = [(dp_of(y, zh, c), dp_of(y, zh, 1 - c)) for y in YS for zh in ZHS for c in CS]
SWAP_ZH = [(dp_of(y, zh, c), dp_of(y, 1 - zh, c)) for y in YS for zh in ZHS for c in CS]


def turn_y(step):
    return [(dp_of(y, zh, c), dp_of((y + step) % NY, zh, c)) for y in YS for zh in ZHS for c in CS]


def turn_x(step):
    return [(tm_of(x, zl), tm_of((x + step) % NX, zl)) for x in XS for zl in ZLS]


def exchange(value, axis, groups=None):
    return lax.all_to_all(value, axis, 0, 0, axis_index_groups=groups, tiled=True)


def split(value):
    high = value.astype(bf16)
    return high, (value - high.astype(f32)).astype(bf16)


NN = (((1,), (0,)), ((), ()))
NT = (((1,), (1,)), ((), ()))


def dot(a, b, dims=NN):
    return lax.dot_general(a, b, dims, preferred_element_type=f32)


def dot3(a, b, dims=NN):
    return dot(a[0], b[0], dims) + (dot(a[0], b[1], dims) + dot(a[1], b[0], dims))


def weights_kernel(place, own, own_other, far, far_other, high, low, held):
    x, y, zh, c = place[0], place[1], place[2], place[3]
    for step in range(NY):
        base = lax.rem(y - step + NY, NY) * (D // NY)
        part = pl.ds(step * 32, 32)
        near = base + zh * 64
        held[pl.ds(pl.multiple_of(near + c * 32, 32), 32), :] = own[part, :]
        held[pl.ds(pl.multiple_of(near + (1 - c) * 32, 32), 32), :] = own_other[part, :]
        away = base + (1 - zh) * 64
        for turn in range(NX):
            inner = lax.rem(x - turn + NX, NX) * 8
            piece = pl.ds(step * 32 + turn * 8, 8)
            held[pl.ds(pl.multiple_of(away + c * 32 + inner, 8), 8), :] = far[piece, :]
            held[pl.ds(pl.multiple_of(away + (1 - c) * 32 + inner, 8), 8), :] = far_other[piece, :]
    for block in range(16):
        rows = pl.ds(block * 32, 32)
        high[rows, :], low[rows, :] = split(held[rows, :])


def take_rows(tiles, rows, count):
    for p in range(OWN):
        for k in range(4):
            rows[p * FRAMES:(p + 1) * FRAMES, k * 128:(k + 1) * 128] = tiles[
                pl.ds(k * 8 + p, FRAMES, stride=count * 8), :
            ]


def to_tiles(rows):
    return rows.reshape(FRAMES, OWN, D // 128, 128).transpose(0, 2, 1, 3)


def head_masks():
    lane = lax.broadcasted_iota(jnp.int32, (HALF, PAIR), 1)
    return lane < HEAD


def forward_kernel(
    slopes, tokens, gain, high, low, spacing,
    emb_out, normt_h, normt_l, qkv_h, qkv_l, weights_out, wt_h, wt_l, mixt_h, mixt_l, pick,
    mixed,
):
    take_rows(tokens, emb_out, 5)
    tags = tokens[pl.ds(32, FRAMES, stride=40), :]
    ids = lax.broadcasted_iota(jnp.int32, (FRAMES, ACTIONS), 1).astype(f32)
    pick[...] = jnp.transpose((tags == ids).astype(f32)).astype(bf16)
    emb = emb_out[...]
    scale = lax.rsqrt(jnp.mean(emb * emb, axis=1, keepdims=True) + 1e-06)
    normed = emb * gain[...] * scale
    normt_h[...], normt_l[...] = split(jnp.transpose(normed))
    parts = split(normed)
    for block in range(QKV // 256):
        cols = slice(block * 256, block * 256 + 256)
        value = dot3(parts, (high[:, cols], low[:, cols]))
        if block < D // 256:
            value = value * 0.125
        qkv_h[:, cols], qkv_l[:, cols] = split(value)
    first = head_masks()
    zero = jnp.zeros((HALF, PAIR), bf16)
    for g in range(2):
        rows = slice(g * HALF, g * HALF + HALF)
        for pair in range(HEADS // 2):
            at = [slice(kind * D + pair * PAIR, kind * D + (pair + 1) * PAIR) for kind in range(3)]
            q, k, v = [(qkv_h[rows, cols], qkv_l[rows, cols]) for cols in at]
            k_twice = jnp.concatenate([k[0], k[0]], axis=1)
            v_all = jnp.concatenate([v[0], v[0], v[1]], axis=0)
            got = []
            for side in range(2):
                keep = first if side == 0 else ~first
                q_h, q_l = jnp.where(keep, q[0], zero), jnp.where(keep, q[1], zero)
                scores = dot(jnp.concatenate([q_h, q_l], axis=1), k_twice, NT) + dot(q_h, k[1], NT)
                scores = scores - slopes[pair * 2 + side] * spacing[...]
                raised = jnp.exp(scores - jnp.max(scores, axis=1, keepdims=True))
                weights = raised * (1.0 / jnp.sum(raised, axis=1, keepdims=True))
                index = (g * 4 + pair) * 2 + side
                weights_out[index] = weights
                wt_h[index], wt_l[index] = split(jnp.transpose(weights))
                w_h, w_l = split(weights)
                got.append(dot(jnp.concatenate([w_h, w_l, w_h], axis=1), v_all))
            mixed[rows, pair * PAIR:(pair + 1) * PAIR] = jnp.where(first, got[0], got[1])
    mixt_h[...], mixt_l[...] = split(jnp.transpose(mixed[...]))


def put_block(place_c, keep_ref, send_ref, block, tile, zero_rows, one_rows):
    mine = place_c == 0
    keep_ref[block, tile] = jnp.where(mine, zero_rows, one_rows)
    send_ref[block, tile] = jnp.where(mine, one_rows, zero_rows)


def backward_kernel(
    place, og_rows, gain, high, low, emb_in, normt_h, normt_l, qkv_h, qkv_l, weights_in,
    wt_h, wt_l, mixt_h, mixt_l, pick,
    keep_ref, send_ref, tokens_out,
    og, gr_h, gr_l,
):
    c = place[3]
    take_rows(og_rows, og, 4)
    og_parts = split(og[...])

    def place_columns(block, value):
        for y in YS:
            for zh in ZHS:
                for x in XS:
                    r = y * 128 + zh * 64 + x * 8
                    for half in range(2):
                        cols = slice(half * 128, half * 128 + 128)
                        put_block(
                            c, keep_ref, send_ref, x * NY + y, (zh * 8 + block) * 2 + half,
                            value[r:r + 8, cols], value[r + 32:r + 40, cols],
                        )

    gm = dot3(og_parts, (high[:, QKV:], low[:, QKV:]), NT)
    gm_h, gm_l = split(gm)
    mixt = (mixt_h[...], mixt_l[...])
    for block in range(2):
        cols = slice(block * 256, block * 256 + 256)
        place_columns(6 + block, dot3(mixt, (og_parts[0][:, cols], og_parts[1][:, cols])))
    first = head_masks()
    zero = jnp.zeros((HALF, PAIR), bf16)
    for g in range(2):
        rows = slice(g * HALF, g * HALF + HALF)
        for pair in range(HEADS // 2):
            at = [slice(kind * D + pair * PAIR, kind * D + (pair + 1) * PAIR) for kind in range(3)]
            q, k, v = [(qkv_h[rows, cols], qkv_l[rows, cols]) for cols in at]
            gmp = (gm_h[rows, at[0]], gm_l[rows, at[0]])
            v_twice = jnp.concatenate([v[0], v[0]], axis=1)
            k_all = jnp.concatenate([k[0], k[0], k[1]], axis=0)
            q_all = jnp.concatenate([q[0], q[0], q[1]], axis=0)
            gm_all = jnp.concatenate([gmp[0], gmp[0], gmp[1]], axis=0)
            dq, dk, dv = [], [], []
            for side in range(2):
                keep = first if side == 0 else ~first
                index = (g * 4 + pair) * 2 + side
                a_h, a_l = jnp.where(keep, gmp[0], zero), jnp.where(keep, gmp[1], zero)
                d_w = dot(jnp.concatenate([a_h, a_l], axis=1), v_twice, NT) + dot(a_h, v[1], NT)
                weights = weights_in[index]
                ds = weights * (d_w - jnp.sum(d_w * weights, axis=1, keepdims=True))
                s_h, s_l = split(ds)
                t_h, t_l = split(jnp.transpose(ds))
                p_h, p_l = wt_h[index], wt_l[index]
                dq.append(dot(jnp.concatenate([s_h, s_l, s_h], axis=1), k_all))
                dk.append(dot(jnp.concatenate([t_h, t_l, t_h], axis=1), q_all))
                dv.append(dot(jnp.concatenate([p_h, p_l, p_h], axis=1), gm_all))
            for cols, pieces, factor in zip(at, (dq, dk, dv), (0.125, 1.0, 1.0)):
                value = jnp.where(first, pieces[0], pieces[1]) * factor
                gr_h[rows, cols], gr_l[rows, cols] = split(value)
    normt = (normt_h[...], normt_l[...])
    for block in range(QKV // 256):
        cols = slice(block * 256, block * 256 + 256)
        place_columns(block, dot3(normt, (gr_h[:, cols], gr_l[:, cols])))
    gn = dot3((gr_h[...], gr_l[...]), (high[:, :QKV], low[:, :QKV]), NT)
    emb = emb_in[...]
    scale = lax.rsqrt(jnp.mean(emb * emb, axis=1, keepdims=True) + 1e-06)
    gain_sum = jnp.sum(gn * emb * scale, axis=0, keepdims=True)
    u = gn * gain[...]
    along = jnp.sum(u * emb, axis=1, keepdims=True) * (scale * scale * scale) * (1.0 / D)
    tokens = og[...] + (u * scale - emb * along)
    total = jnp.zeros((FRAMES, D), f32)
    for p in range(OWN):
        piece = tokens[p * FRAMES:(p + 1) * FRAMES, :]
        for k in range(4):
            tokens_out[pl.ds(k * 8 + p, FRAMES, stride=32), :] = piece[:, k * 128:(k + 1) * 128]
        total = total + piece
    total_h, total_l = split(total)
    table = dot(pick[...], total_h) + dot(pick[...], total_l)
    for block in range(16):
        r = slice(block * 8, block * 8 + 8)
        for half in range(2):
            left = slice(half * 128, half * 128 + 128)
            right = slice(256 + half * 128, 256 + half * 128 + 128)
            put_block(c, keep_ref, send_ref, block, 32 + half, table[r, left], table[r, right])
    gain_tile = jnp.concatenate(
        [gain_sum[:, i * 128:(i + 1) * 128] for i in range(4)] + [jnp.zeros((4, 128), f32)], axis=0
    )
    for block in range(16):
        keep_ref[block, 34] = gain_tile
        send_ref[block, 34] = gain_tile


def call(kernel, outs, scratch, scalars, *arrays, name):
    vmem = pl.BlockSpec(memory_space=pltpu.VMEM)
    smem = pl.BlockSpec(memory_space=pltpu.SMEM)
    return pl.pallas_call(
        kernel,
        out_shape=outs,
        in_specs=[smem] * len(scalars) + [vmem] * len(arrays),
        out_specs=jax.tree.map(lambda _: vmem, outs),
        scratch_shapes=scratch,
        compiler_params=pltpu.CompilerParams(vmem_limit_bytes=48 * 1024 * 1024),
        name=name,
    )(*scalars, *arrays)


def shape(*dims, kind=f32):
    return jax.ShapeDtypeStruct(dims, kind)


def gathered_weights(w_qkv, w_out, x, place):
    mine = jnp.concatenate([w_qkv, w_out], axis=1)
    quarter = lax.dynamic_slice(mine, (x * 8, 0), (8, mine.shape[1]))
    quarter = lax.ppermute(quarter, "dp", SWAP_ZH)
    far = jnp.concatenate(
        [quarter] + [lax.ppermute(quarter, "tm", turn_x(step)) for step in range(1, NX)], axis=0
    )

    def along_y(rows):
        return jnp.concatenate(
            [rows] + [lax.ppermute(rows, "dp", turn_y(step)) for step in range(1, NY)], axis=0
        )

    own_all, far_all = along_y(mine), along_y(far)
    own_other = lax.ppermute(own_all, "dp", SWAP_CORE)
    far_other = lax.ppermute(far_all, "dp", SWAP_CORE)
    return call(
        weights_kernel,
        (shape(D, QKV + D, kind=bf16),) * 2,
        [pltpu.VMEM((D, QKV + D), f32)],
        (place,),
        own_all, own_other, far_all, far_other,
        name="weights",
    )


def shards(
    video_tokens, actions, frame_times, act_table, norm_gain, w_qkv, w_out, slopes, out_grad
):
    t, d = lax.axis_index("tm"), lax.axis_index("dp")
    x, y, zh, c = t // NZL, d // (NZH * NC), (d // NC) % NZH, d % NC
    place = jnp.stack([x, y, zh, c]).astype(jnp.int32)
    gain = norm_gain.reshape(1, D)

    action = actions[0, 0]
    row = lax.dynamic_slice(act_table, (action, 0), (1, D))
    embedded = to_tiles(video_tokens[0, 0] + row)
    tag = jnp.broadcast_to(action.astype(f32), (FRAMES, 1, OWN, ACTIONS))
    tokens = exchange(jnp.concatenate([embedded, tag], axis=1), "tm")
    og = exchange(to_tiles(out_grad[0, 0]), "tm")
    high, low = gathered_weights(w_qkv, w_out, x, place)

    times = jnp.tile(frame_times[0].astype(f32), HALF // FRAMES)
    i = lax.broadcasted_iota(jnp.int32, (HALF, HALF), 0)
    j = lax.broadcasted_iota(jnp.int32, (HALF, HALF), 1)
    seen = (i // FRAMES == j // FRAMES) & (j <= i)
    spacing = jnp.where(seen, times[:, None] - times[None, :], f32(1e30))

    kept = call(
        forward_kernel,
        (
            shape(ROWS, D), shape(D, ROWS, kind=bf16), shape(D, ROWS, kind=bf16),
            shape(ROWS, QKV, kind=bf16), shape(ROWS, QKV, kind=bf16),
            shape(16, HALF, HALF), shape(16, HALF, HALF, kind=bf16),
            shape(16, HALF, HALF, kind=bf16),
            shape(D, ROWS, kind=bf16), shape(D, ROWS, kind=bf16),
            shape(ACTIONS, FRAMES, kind=bf16),
        ),
        [pltpu.VMEM((ROWS, D), f32)],
        (slopes,),
        tokens.reshape(ROWS * 5, 128), gain, high, low, spacing,
        name="forward",
    )
    keep, send, tokens_back = call(
        backward_kernel,
        (shape(16, TILES, 8, 128), shape(16, TILES, 8, 128), shape(ROWS * 4, 128)),
        [
            pltpu.VMEM((ROWS, D), f32),
            pltpu.VMEM((ROWS, QKV), bf16),
            pltpu.VMEM((ROWS, QKV), bf16),
        ],
        (place,),
        og.reshape(ROWS * 4, 128), gain, high, low, *kept,
        name="backward",
    )
    grad_tokens = exchange(tokens_back.reshape(FRAMES, 4, OWN, 128), "tm")

    both_cores = keep + lax.ppermute(send, "dp", SWAP_CORE)
    plane = jnp.sum(exchange(both_cores, BOTH, XY_GROUPS), axis=0)
    column = jnp.concatenate(
        [plane[:32].reshape(16, 2, 8, 128), jnp.broadcast_to(plane[32:], (16, 3, 8, 128))], axis=1
    )
    total = jnp.sum(exchange(column, BOTH, Z_GROUPS), axis=0)

    line = exchange(jnp.broadcast_to(total[:2], (NZL, 2, 8, 128)), "tm", ZL_GROUPS)
    table = total[2:4]
    turned = jnp.stack(
        [table] + [lax.ppermute(table, "dp", turn_y(step)) for step in range(1, NY)]
    )
    table_y = jnp.take(turned, (y - jnp.arange(NY)) % NY, axis=0)
    block = jnp.concatenate([line.reshape(16, 8, 128), table_y.reshape(8, 8, 128)], axis=0)
    sheet = exchange(jnp.broadcast_to(block, (NX, 24, 8, 128)), "tm", X_GROUPS)
    shares = sheet.reshape(NX, 24, 8, 128)
    main = shares[:, :16].transpose(0, 2, 1, 3).reshape(32, QKV + D)
    half = shares[:, 16:].reshape(16, 2, 8, 128).transpose(0, 2, 1, 3).reshape(ACTIONS, 256)
    other = lax.ppermute(half, "dp", SWAP_CORE)
    grad_table = jnp.where(
        c == 0, jnp.concatenate([half, other], axis=1), jnp.concatenate([other, half], axis=1)
    )
    return (
        grad_tokens.transpose(0, 2, 1, 3).reshape(1, 1, ROWS, D),
        main[:, :QKV],
        main[:, QKV:],
        grad_table,
        total[4, :4].reshape(D),
    )


def solution(mesh):
    return jax.shard_map(
        shards,
        mesh=mesh,
        in_specs=(
            P("dp", "tm", None, None),
            P("dp", "tm"),
            P("dp", None),
            P(),
            P(),
            P("dp", None),
            P("dp", None),
            P(),
            P("dp", "tm", None, None),
        ),
        out_specs=(P("dp", "tm", None, None), P("dp", None), P("dp", None), P(), P()),
        check_vma=False,
    )
```

```python
import functools

import jax
import jax.numpy as jnp
from jax import lax
from jax.experimental import pallas as pl
from jax.experimental.pallas import tpu as pltpu
from jax.sharding import PartitionSpec as P

NX, NZL, NY, NZH, NC = 4, 8, 4, 2, 2
D, QKV, HEADS, HEAD, FRAMES, OWN = 512, 1536, 8, 64, 32, 8
ROWS = FRAMES * OWN
HALF = ROWS // 2
PAIR = 2 * HEAD
ACTIONS = 128
TILES = 41
f32, bf16 = jnp.float32, jnp.bfloat16
BOTH = ("tm", "dp")


def tm_of(x, zl):
    return x * NZL + zl


def dp_of(y, zh, c):
    return (y * NZH + zh) * NC + c


def flat_of(x, zl, y, zh, c):
    return tm_of(x, zl) * (NY * NZH * NC) + dp_of(y, zh, c)


XS, ZLS, YS, ZHS, CS = range(NX), range(NZL), range(NY), range(NZH), range(NC)
X_GROUPS = [[tm_of(x, zl) for x in XS] for zl in ZLS]
ZL_GROUPS = [[tm_of(x, zl) for zl in ZLS] for x in XS]
YC_GROUPS = [[dp_of(y, zh, c) for y in YS for c in CS] for zh in ZHS]
Z_GROUPS = [
    [flat_of(x, zl, y, zh, c) for zh in ZHS for zl in ZLS] for x in XS for y in YS for c in CS
]
SWAP_CORE = [(dp_of(y, zh, c), dp_of(y, zh, 1 - c)) for y in YS for zh in ZHS for c in CS]
SWAP_ZH = [(dp_of(y, zh, c), dp_of(y, 1 - zh, c)) for y in YS for zh in ZHS for c in CS]


def turn_y(step):
    return [(dp_of(y, zh, c), dp_of((y + step) % NY, zh, c)) for y in YS for zh in ZHS for c in CS]


def turn_x(step):
    return [(tm_of(x, zl), tm_of((x + step) % NX, zl)) for x in XS for zl in ZLS]


def exchange(value, axis, groups=None):
    return lax.all_to_all(value, axis, 0, 0, axis_index_groups=groups, tiled=True)


def split(value):
    high = value.astype(bf16)
    return high, (value - high.astype(f32)).astype(bf16)


NN = (((1,), (0,)), ((), ()))
NT = (((1,), (1,)), ((), ()))


def dot(a, b, dims=NN):
    return lax.dot_general(a, b, dims, preferred_element_type=f32)


def dot3(a, b, dims=NN):
    return dot(a[0], b[0], dims) + (dot(a[0], b[1], dims) + dot(a[1], b[0], dims))


def take_rows(tiles, rows, start):
    for p in range(OWN):
        for k in range(4):
            rows[p * FRAMES:(p + 1) * FRAMES, k * 128:(k + 1) * 128] = tiles[
                pl.ds((start + k) * 8 + p, FRAMES, stride=72), :
            ]


def to_tiles(rows):
    return rows.reshape(FRAMES, OWN, D // 128, 128).transpose(0, 2, 1, 3)


def head_masks():
    lane = lax.broadcasted_iota(jnp.int32, (HALF, PAIR), 1)
    return lane < HEAD


def gather_weights(place, own, far_mine, far_other, high, low):
    x, y, zh, c = place[0], place[1], place[2], place[3]
    for y_to in YS:
        for side in CS:
            at = pl.ds(pl.multiple_of(y_to * 128 + zh * 64 + side * 32, 32), 32)
            high[at, :], low[at, :] = split(own[y_to * 2 + side])
        turn_y = lax.rem(y - y_to + NY, NY) * NX
        for x_to in range(0, NX, 2):
            turns = [turn_y + lax.rem(x - x_to - i + NX, NX) for i in range(2)]
            for side, ref in ((c, far_mine), (1 - c, far_other)):
                rows = jnp.concatenate([ref[turn] for turn in turns], axis=0)
                at = y_to * 128 + (1 - zh) * 64 + side * 32 + x_to * 8
                at = pl.ds(pl.multiple_of(at, 16), 16)
                high[at, :], low[at, :] = split(rows)


def sublayer_kernel(
    place, slopes, tiles, gain, own, far_mine, far_other, spacing,
    grads, tokens_out,
    high, low, emb_ref, og, qkv_h, qkv_l, gm_h, gm_l, mixed, gr_h, gr_l,
):
    take_rows(tiles, emb_ref, 0)
    take_rows(tiles, og, 4)
    gather_weights(place, own, far_mine, far_other, high, low)

    tags = tiles[pl.ds(64, FRAMES, stride=72), :]
    ids = lax.broadcasted_iota(jnp.int32, (FRAMES, ACTIONS), 1).astype(f32)
    pick = jnp.transpose((tags == ids).astype(f32)).astype(bf16)

    emb = emb_ref[...]
    scale = lax.rsqrt(jnp.mean(emb * emb, axis=1, keepdims=True) + 1e-06)
    normed = emb * gain[...] * scale
    parts = split(normed)
    for block in range(QKV // 256):
        cols = slice(block * 256, block * 256 + 256)
        value = dot3(parts, (high[:, cols], low[:, cols]))
        if block < D // 256:
            value = value * 0.125
        qkv_h[:, cols], qkv_l[:, cols] = split(value)
    og_parts = split(og[...])
    gm_h[...], gm_l[...] = split(dot3(og_parts, (high[:, QKV:], low[:, QKV:]), NT))

    lane = lax.broadcasted_iota(jnp.int32, (ROWS, PAIR), 1) < HEAD
    upper = lax.broadcasted_iota(jnp.int32, (ROWS, PAIR), 0) < HALF
    own_half = lane == upper
    first = lane[:HALF]
    zero = jnp.zeros((ROWS, PAIR), bf16)

    def both_heads(parts):
        twice = [jnp.where(own_half, jnp.concatenate([v, v], axis=0), zero) for v in parts]
        return jnp.concatenate([twice[0], twice[1], twice[0]], axis=1)

    def wide(parts):
        return jnp.concatenate([parts[0], parts[0], parts[1]], axis=1)

    def tall(parts):
        return jnp.concatenate([parts[0], parts[0], parts[1]], axis=0)

    def left(value):
        high_part, low_part = split(value)
        return jnp.concatenate([high_part, low_part, high_part], axis=1)

    def turned(value):
        return jnp.concatenate([jnp.transpose(value[:HALF]), jnp.transpose(value[HALF:])], axis=0)

    def pick_lanes(value):
        return jnp.where(first, value[:HALF], value[HALF:])

    for pair in range(HEADS // 2):
        slope = jnp.concatenate(
            [slopes[pair * 2] * spacing[...], slopes[pair * 2 + 1] * spacing[...]], axis=0
        )
        at = [slice(kind * D + pair * PAIR, kind * D + (pair + 1) * PAIR) for kind in range(3)]
        for g in range(2):
            rows = slice(g * HALF, g * HALF + HALF)
            q, k, v = [(qkv_h[rows, cols], qkv_l[rows, cols]) for cols in at]
            gmp = (gm_h[rows, at[0]], gm_l[rows, at[0]])
            scores = dot(both_heads(q), wide(k), NT) - slope
            raised = jnp.exp(scores - jnp.max(scores, axis=1, keepdims=True))
            weights = raised * (1.0 / jnp.sum(raised, axis=1, keepdims=True))
            d_w = dot(both_heads(gmp), wide(v), NT)
            ds = weights * (d_w - jnp.sum(d_w * weights, axis=1, keepdims=True))
            mixed[rows, at[0]] = pick_lanes(dot(left(weights), tall(v)))
            dq = pick_lanes(dot(left(ds), tall(k))) * 0.125
            dk = pick_lanes(dot(left(turned(ds)), tall(q)))
            dv = pick_lanes(dot(left(turned(weights)), tall(gmp)))
            for cols, value in zip(at, (dq, dk, dv)):
                gr_h[rows, cols], gr_l[rows, cols] = split(value)

    def place_columns(block, value):
        for y in YS:
            for side in CS:
                for x in XS:
                    for zh in ZHS:
                        r = y * 128 + zh * 64 + side * 32 + x * 8
                        for half in range(2):
                            grads[y * 2 + side, x, (zh * 8 + block) * 2 + half] = value[
                                r:r + 8, half * 128:half * 128 + 128
                            ]

    normt = split(jnp.transpose(normed))
    for block in range(QKV // 256):
        cols = slice(block * 256, block * 256 + 256)
        place_columns(block, dot3(normt, (gr_h[:, cols], gr_l[:, cols])))
    mixt = split(jnp.transpose(mixed[...]))
    for block in range(2):
        cols = slice(block * 256, block * 256 + 256)
        place_columns(6 + block, dot3(mixt, (og_parts[0][:, cols], og_parts[1][:, cols])))

    gn = dot3((gr_h[...], gr_l[...]), (high[:, :QKV], low[:, :QKV]), NT)
    gain_sum = jnp.sum(gn * emb * scale, axis=0, keepdims=True)
    u = gn * gain[...]
    along = jnp.sum(u * emb, axis=1, keepdims=True) * (scale * scale * scale) * (1.0 / D)
    tokens = og[...] + (u * scale - emb * along)
    total = jnp.zeros((FRAMES, D), f32)
    for p in range(OWN):
        piece = tokens[p * FRAMES:(p + 1) * FRAMES, :]
        for k in range(4):
            tokens_out[pl.ds(k * 8 + p, FRAMES, stride=32), :] = piece[:, k * 128:(k + 1) * 128]
        total = total + piece
    total_h, total_l = split(total)
    table = dot(pick, total_h) + dot(pick, total_l)
    gain_tile = jnp.concatenate(
        [gain_sum[:, i * 128:(i + 1) * 128] for i in range(4)] + [jnp.zeros((4, 128), f32)], axis=0
    )
    for x in XS:
        for side in CS:
            for k in range(8):
                r, start = x * 32 + (k // 2) * 8, side * 256 + (k % 2) * 128
                for y in YS:
                    grads[y * 2 + side, x, 32 + k] = table[r:r + 8, start:start + 128]
            for y in YS:
                grads[y * 2 + side, x, 40] = gain_tile


def call(kernel, outs, scratch, scalars, *arrays, name):
    vmem = pl.BlockSpec(memory_space=pltpu.VMEM)
    smem = pl.BlockSpec(memory_space=pltpu.SMEM)
    return pl.pallas_call(
        kernel,
        out_shape=outs,
        in_specs=[smem] * len(scalars) + [vmem] * len(arrays),
        out_specs=jax.tree.map(lambda _: vmem, outs),
        scratch_shapes=scratch,
        compiler_params=pltpu.CompilerParams(vmem_limit_bytes=48 * 1024 * 1024),
        name=name,
    )(*scalars, *arrays)


def shape(*dims, kind=f32):
    return jax.ShapeDtypeStruct(dims, kind)


def gathered_weights(w_qkv, w_out, x):
    mine = jnp.concatenate([w_qkv, w_out], axis=1)
    own = lax.all_gather(mine, "dp", axis_index_groups=YC_GROUPS)
    quarter = lax.ppermute(lax.dynamic_slice(mine, (x * 8, 0), (8, QKV + D)), "dp", SWAP_ZH)
    return own, quarter


def far_weights(quarter):
    row = jnp.stack([quarter] + [lax.ppermute(quarter, "tm", turn_x(i)) for i in range(1, NX)])
    far = jnp.concatenate([row] + [lax.ppermute(row, "dp", turn_y(i)) for i in range(1, NY)])
    return far, lax.ppermute(far, "dp", SWAP_CORE)


def shards(
    video_tokens, actions, frame_times, act_table, norm_gain, w_qkv, w_out, slopes, out_grad
):
    t, d = lax.axis_index("tm"), lax.axis_index("dp")
    x, y, zh, c = t // NZL, d // (NZH * NC), (d // NC) % NZH, d % NC
    place = jnp.stack([x, y, zh, c]).astype(jnp.int32)

    own, quarter = gathered_weights(w_qkv, w_out, x)
    action = actions[0, 0]
    row = lax.dynamic_slice(act_table, (action, 0), (1, D))
    tag = jnp.broadcast_to(action.astype(f32), (FRAMES, 1, OWN, ACTIONS))
    payload = jnp.concatenate(
        [to_tiles(video_tokens[0, 0] + row), to_tiles(out_grad[0, 0]), tag], axis=1
    )
    quarter, payload = lax.optimization_barrier((quarter, payload))
    tiles = exchange(payload, "tm")
    weights = (own, *far_weights(quarter))

    times = jnp.tile(frame_times[0].astype(f32), HALF // FRAMES)
    i = lax.broadcasted_iota(jnp.int32, (HALF, HALF), 0)
    j = lax.broadcasted_iota(jnp.int32, (HALF, HALF), 1)
    seen = (i // FRAMES == j // FRAMES) & (j <= i)
    spacing = jnp.where(seen, times[:, None] - times[None, :], f32(1e30))

    grads, tokens_back = call(
        sublayer_kernel,
        (shape(NY * NC, NX, TILES, 8, 128), shape(ROWS * 4, 128)),
        [
            pltpu.VMEM((D, QKV + D), bf16), pltpu.VMEM((D, QKV + D), bf16),
            pltpu.VMEM((ROWS, D), f32), pltpu.VMEM((ROWS, D), f32),
            pltpu.VMEM((ROWS, QKV), bf16), pltpu.VMEM((ROWS, QKV), bf16),
            pltpu.VMEM((ROWS, D), bf16), pltpu.VMEM((ROWS, D), bf16),
            pltpu.VMEM((ROWS, D), f32),
            pltpu.VMEM((ROWS, QKV), bf16), pltpu.VMEM((ROWS, QKV), bf16),
        ],
        (place, slopes),
        tiles.reshape(ROWS * 9, 128), norm_gain.reshape(1, D), *weights, spacing,
        name="sublayer",
    )
    grad_tokens = exchange(tokens_back.reshape(FRAMES, 4, OWN, 128), "tm")

    row = lax.psum_scatter(
        grads, "dp", scatter_dimension=0, axis_index_groups=YC_GROUPS, tiled=True
    ).reshape(NX, TILES, 8, 128)
    row, grad_tokens = lax.optimization_barrier((row, grad_tokens))
    plane = jnp.sum(exchange(row, "tm", X_GROUPS), axis=0)
    column = jnp.concatenate(
        [
            plane[:32].reshape(16, 2, 8, 128),
            jnp.tile(plane[32:40], (2, 1, 1)).reshape(16, 1, 8, 128),
            jnp.broadcast_to(plane[40:], (16, 1, 8, 128)),
        ],
        axis=1,
    )
    total = jnp.sum(exchange(column, BOTH, Z_GROUPS), axis=0)

    line = exchange(jnp.broadcast_to(total[:3], (NZL, 3, 8, 128)), "tm", ZL_GROUPS)
    sheet = exchange(jnp.broadcast_to(line, (NX, NZL, 3, 8, 128)), "tm", X_GROUPS)
    main = sheet[:, :, :2].transpose(0, 3, 1, 2, 4).reshape(32, QKV + D)
    half = sheet[:, :, 2].reshape(NX, 4, 2, 8, 128).transpose(0, 1, 3, 2, 4).reshape(ACTIONS, 256)
    other = lax.ppermute(half, "dp", SWAP_CORE)
    grad_table = jnp.where(
        c == 0, jnp.concatenate([half, other], axis=1), jnp.concatenate([other, half], axis=1)
    )
    return (
        grad_tokens.transpose(0, 2, 1, 3).reshape(1, 1, ROWS, D),
        main[:, :QKV],
        main[:, QKV:],
        grad_table,
        total[3, :4].reshape(D),
    )


def solution(mesh):
    return jax.shard_map(
        shards,
        mesh=mesh,
        in_specs=(
            P("dp", "tm", None, None),
            P("dp", "tm"),
            P("dp", None),
            P(),
            P(),
            P("dp", None),
            P("dp", None),
            P(),
            P("dp", "tm", None, None),
        ),
        out_specs=(P("dp", "tm", None, None), P("dp", None), P("dp", None), P(), P()),
        check_vma=False,
    )
```

```python
import functools

import jax
import jax.numpy as jnp
from jax import lax
from jax.experimental import pallas as pl
from jax.experimental.pallas import tpu as pltpu
from jax.sharding import PartitionSpec as P

NX, NZL, NY, NZH, NC = 4, 8, 4, 2, 2
D, QKV, HEADS, HEAD, FRAMES, OWN = 512, 1536, 8, 64, 32, 8
ROWS = FRAMES * OWN
HALF = ROWS // 2
PAIR = 2 * HEAD
ACTIONS = 128
TILES = 41
CHUNK = 65
f32, bf16 = jnp.float32, jnp.bfloat16
BOTH = ("tm", "dp")


def tm_of(x, zl):
    return x * NZL + zl


def dp_of(y, zh, c):
    return (y * NZH + zh) * NC + c


def flat_of(x, zl, y, zh, c):
    return tm_of(x, zl) * (NY * NZH * NC) + dp_of(y, zh, c)


XS, ZLS, YS, ZHS, CS = range(NX), range(NZL), range(NY), range(NZH), range(NC)
X_GROUPS = [[tm_of(x, zl) for x in XS] for zl in ZLS]
ZL_GROUPS = [[tm_of(x, zl) for zl in ZLS] for x in XS]
YC_GROUPS = [[dp_of(y, zh, c) for y in YS for c in CS] for zh in ZHS]
Z_GROUPS = [
    [flat_of(x, zl, y, zh, c) for zh in ZHS for zl in ZLS] for x in XS for y in YS for c in CS
]
SWAP_CORE = [(dp_of(y, zh, c), dp_of(y, zh, 1 - c)) for y in YS for zh in ZHS for c in CS]
SWAP_ZH = [(dp_of(y, zh, c), dp_of(y, 1 - zh, c)) for y in YS for zh in ZHS for c in CS]


def turn_y(step):
    return [(dp_of(y, zh, c), dp_of((y + step) % NY, zh, c)) for y in YS for zh in ZHS for c in CS]


def turn_x(step):
    return [(tm_of(x, zl), tm_of((x + step) % NX, zl)) for x in XS for zl in ZLS]


def exchange(value, axis, groups=None):
    return lax.all_to_all(value, axis, 0, 0, axis_index_groups=groups, tiled=True)


def split(value):
    high = value.astype(bf16)
    return high, (value - high.astype(f32)).astype(bf16)


NN = (((1,), (0,)), ((), ()))
NT = (((1,), (1,)), ((), ()))


def dot(a, b, dims=NN):
    return lax.dot_general(a, b, dims, preferred_element_type=f32)


def dot3(a, b, dims=NN):
    return dot(a[0], b[0], dims) + (dot(a[0], b[1], dims) + dot(a[1], b[0], dims))


def take_rows(tiles, rows, start):
    for p in range(OWN):
        for k in range(4):
            rows[p * FRAMES:(p + 1) * FRAMES, k * 128:(k + 1) * 128] = tiles[
                pl.ds((start + k) * 8 + p, FRAMES, stride=CHUNK), :
            ]


def pack_kernel(action, row, video_in, og_in, out, video, og, sems):
    arrivals = [
        pltpu.make_async_copy(source, target, sems.at[i])
        for i, (source, target) in enumerate(((video_in, video), (og_in, og)))
    ]
    for copy in arrivals:
        copy.start()
    for copy in arrivals:
        copy.wait()
    tag = jnp.zeros((1, 128), f32) + action[0].astype(f32)
    for f in range(FRAMES):
        rows = slice(f * OWN, f * OWN + OWN)
        for k in range(D // 128):
            cols = slice(k * 128, k * 128 + 128)
            out[f * CHUNK + k * 8:f * CHUNK + k * 8 + 8, :] = video[rows, cols] + row[:, cols]
            out[f * CHUNK + 32 + k * 8:f * CHUNK + 40 + k * 8, :] = og[rows, cols]
        out[f * CHUNK + 64:f * CHUNK + 65, :] = tag


def weights_kernel(place, own, far_mine, far_other, high, low):
    x, y, zh, c = place[0], place[1], place[2], place[3]
    for y_to in YS:
        for side in CS:
            at = pl.ds(pl.multiple_of(y_to * 128 + zh * 64 + side * 32, 32), 32)
            high[at, :], low[at, :] = split(own[y_to * 2 + side])
        turn_y = lax.rem(y - y_to + NY, NY) * NX
        for x_to in range(0, NX, 2):
            turns = [turn_y + lax.rem(x - x_to - i + NX, NX) for i in range(2)]
            for side, ref in ((c, far_mine), (1 - c, far_other)):
                rows = jnp.concatenate([ref[turn] for turn in turns], axis=0)
                at = y_to * 128 + (1 - zh) * 64 + side * 32 + x_to * 8
                at = pl.ds(pl.multiple_of(at, 16), 16)
                high[at, :], low[at, :] = split(rows)


def sublayer_kernel(
    slopes, tiles, gain, spacing, high_in, low_in,
    grads_out, tokens_out,
    grads, tokens_new, sems, high, low, emb_ref, og, qkv_h, qkv_l, gm_h, gm_l, mixed, gr_h, gr_l,
):
    arrivals = [
        pltpu.make_async_copy(source, target, sems.at[18 + i])
        for i, (source, target) in enumerate(((high_in, high), (low_in, low)))
    ]
    for copy in arrivals:
        copy.start()
    take_rows(tiles, emb_ref, 0)
    take_rows(tiles, og, 4)

    tags = tiles[pl.ds(64, FRAMES, stride=CHUNK), :]
    ids = lax.broadcasted_iota(jnp.int32, (FRAMES, ACTIONS), 1).astype(f32)
    pick = jnp.transpose((tags == ids).astype(f32)).astype(bf16)

    emb = emb_ref[...]
    scale = lax.rsqrt(jnp.mean(emb * emb, axis=1, keepdims=True) + 1e-06)
    normed = emb * gain[...] * scale
    parts = split(normed)
    for copy in arrivals:
        copy.wait()
    for block in range(QKV // 256):
        cols = slice(block * 256, block * 256 + 256)
        value = dot3(parts, (high[:, cols], low[:, cols]))
        if block < D // 256:
            value = value * 0.125
        qkv_h[:, cols], qkv_l[:, cols] = split(value)
    og_parts = split(og[...])
    gm_h[...], gm_l[...] = split(dot3(og_parts, (high[:, QKV:], low[:, QKV:]), NT))

    lane = lax.broadcasted_iota(jnp.int32, (ROWS, PAIR), 1) < HEAD
    upper = lax.broadcasted_iota(jnp.int32, (ROWS, PAIR), 0) < HALF
    own_half = lane == upper
    first = lane[:HALF]
    zero = jnp.zeros((ROWS, PAIR), bf16)

    def both_heads(parts):
        twice = [jnp.where(own_half, jnp.concatenate([v, v], axis=0), zero) for v in parts]
        return jnp.concatenate([twice[0], twice[1], twice[0]], axis=1)

    def wide(parts):
        return jnp.concatenate([parts[0], parts[0], parts[1]], axis=1)

    def tall(parts):
        return jnp.concatenate([parts[0], parts[0], parts[1]], axis=0)

    def left(value):
        high_part, low_part = split(value)
        return jnp.concatenate([high_part, low_part, high_part], axis=1)

    def turned(value):
        return jnp.concatenate([jnp.transpose(value[:HALF]), jnp.transpose(value[HALF:])], axis=0)

    def pick_lanes(value):
        return jnp.where(first, value[:HALF], value[HALF:])

    for pair in range(HEADS // 2):
        slope = jnp.concatenate(
            [slopes[pair * 2] * spacing[...], slopes[pair * 2 + 1] * spacing[...]], axis=0
        )
        at = [slice(kind * D + pair * PAIR, kind * D + (pair + 1) * PAIR) for kind in range(3)]
        for g in range(2):
            rows = slice(g * HALF, g * HALF + HALF)
            q, k, v = [(qkv_h[rows, cols], qkv_l[rows, cols]) for cols in at]
            gmp = (gm_h[rows, at[0]], gm_l[rows, at[0]])
            scores = dot(both_heads(q), wide(k), NT) - slope
            raised = jnp.exp(scores - jnp.max(scores, axis=1, keepdims=True))
            weights = raised * (1.0 / jnp.sum(raised, axis=1, keepdims=True))
            d_w = dot(both_heads(gmp), wide(v), NT)
            ds = weights * (d_w - jnp.sum(d_w * weights, axis=1, keepdims=True))
            mixed[rows, at[0]] = pick_lanes(dot(left(weights), tall(v)))
            dq = pick_lanes(dot(left(ds), tall(k))) * 0.125
            dk = pick_lanes(dot(left(turned(ds)), tall(q)))
            dv = pick_lanes(dot(left(turned(weights)), tall(gmp)))
            for cols, value in zip(at, (dq, dk, dv)):
                gr_h[rows, cols], gr_l[rows, cols] = split(value)

    def copy_tiles(tile, count, index):
        part = (slice(None), slice(None), pl.ds(tile, count))
        return pltpu.make_async_copy(grads.at[part], grads_out.at[part], sems.at[index])

    copies = []

    def send_tiles(tile, count, index):
        copies.append(copy_tiles(tile, count, index))
        copies[-1].start()

    def place_columns(block, value):
        for y in YS:
            for side in CS:
                for x in XS:
                    for zh in ZHS:
                        r = y * 128 + zh * 64 + side * 32 + x * 8
                        for half in range(2):
                            grads[y * 2 + side, x, (zh * 8 + block) * 2 + half] = value[
                                r:r + 8, half * 128:half * 128 + 128
                            ]
        for zh in ZHS:
            send_tiles((zh * 8 + block) * 2, 2, block * 2 + zh)

    normt = split(jnp.transpose(normed))
    for block in range(QKV // 256):
        cols = slice(block * 256, block * 256 + 256)
        place_columns(block, dot3(normt, (gr_h[:, cols], gr_l[:, cols])))
    mixt = split(jnp.transpose(mixed[...]))
    for block in range(2):
        cols = slice(block * 256, block * 256 + 256)
        place_columns(6 + block, dot3(mixt, (og_parts[0][:, cols], og_parts[1][:, cols])))

    gn = dot3((gr_h[...], gr_l[...]), (high[:, :QKV], low[:, :QKV]), NT)
    gain_sum = jnp.sum(gn * emb * scale, axis=0, keepdims=True)
    u = gn * gain[...]
    along = jnp.sum(u * emb, axis=1, keepdims=True) * (scale * scale * scale) * (1.0 / D)
    tokens = og[...] + (u * scale - emb * along)
    total = jnp.zeros((FRAMES, D), f32)
    for p in range(OWN):
        piece = tokens[p * FRAMES:(p + 1) * FRAMES, :]
        for k in range(4):
            tokens_new[pl.ds(k * 8 + p, FRAMES, stride=32), :] = piece[:, k * 128:(k + 1) * 128]
        total = total + piece
    copies.append(pltpu.make_async_copy(tokens_new, tokens_out, sems.at[17]))
    copies[-1].start()
    total_h, total_l = split(total)
    table = dot(pick, total_h) + dot(pick, total_l)
    gain_tile = jnp.concatenate(
        [gain_sum[:, i * 64:(i + 1) * 64] for i in range(8)], axis=0
    )
    gain_tile = jnp.concatenate([gain_tile, jnp.zeros((8, 64), f32)], axis=1
    )
    for x in XS:
        for side in CS:
            for k in range(8):
                r, start = x * 32 + (k // 2) * 8, side * 256 + (k % 2) * 128
                for y in YS:
                    grads[y * 2 + side, x, 32 + k] = table[r:r + 8, start:start + 128]
            for y in YS:
                grads[y * 2 + side, x, 40] = gain_tile
    send_tiles(32, 9, 16)
    for copy in copies:
        copy.wait()


def call(kernel, outs, scratch, scalars, *arrays, name, far_ins=0, far_outs=0, limit=24):
    vmem = pl.BlockSpec(memory_space=pltpu.VMEM)
    smem = pl.BlockSpec(memory_space=pltpu.SMEM)
    hbm = pl.BlockSpec(memory_space=pltpu.HBM)
    return pl.pallas_call(
        kernel,
        out_shape=outs,
        in_specs=[smem] * len(scalars) + [vmem] * (len(arrays) - far_ins) + [hbm] * far_ins,
        out_specs=[hbm] * far_outs + [vmem] * (len(outs) - far_outs),
        scratch_shapes=scratch,
        compiler_params=pltpu.CompilerParams(vmem_limit_bytes=limit * 1024 * 1024),
        name=name,
    )(*scalars, *arrays)


def shape(*dims, kind=f32):
    return jax.ShapeDtypeStruct(dims, kind)


def gathered_weights(w_qkv, w_out, x):
    mine = jnp.concatenate([w_qkv, w_out], axis=1)
    own = lax.all_gather(mine, "dp", axis_index_groups=YC_GROUPS)
    quarter = jnp.concatenate(
        [lax.dynamic_slice(w, (x * 8, 0), (8, w.shape[1])) for w in (w_qkv, w_out)], axis=1
    )
    quarter = lax.ppermute(quarter, "dp", SWAP_ZH)
    return own, quarter


def far_weights(own, quarter):
    row = jnp.stack([quarter] + [lax.ppermute(quarter, "tm", turn_x(i)) for i in range(1, NX)])
    row, own = lax.optimization_barrier((row, own))
    far = jnp.concatenate([row] + [lax.ppermute(row, "dp", turn_y(i)) for i in range(1, NY)])
    return own, far, lax.ppermute(far, "dp", SWAP_CORE)


def shards(
    video_tokens, actions, frame_times, act_table, norm_gain, w_qkv, w_out, slopes, out_grad
):
    t, d = lax.axis_index("tm"), lax.axis_index("dp")
    x, y, zh, c = t // NZL, d // (NZH * NC), (d // NC) % NZH, d % NC
    place = jnp.stack([x, y, zh, c]).astype(jnp.int32)

    own, quarter = gathered_weights(w_qkv, w_out, x)
    action = actions[0, 0]
    row = lax.dynamic_slice(act_table, (action, 0), (1, D))
    payload = call(
        pack_kernel,
        [shape(FRAMES * CHUNK, 128)],
        [pltpu.VMEM((ROWS, D), f32), pltpu.VMEM((ROWS, D), f32), pltpu.SemaphoreType.DMA((2,))],
        (action.reshape(1),),
        row, video_tokens[0, 0], out_grad[0, 0],
        name="pack", far_ins=2,
    )[0]
    quarter, payload = lax.optimization_barrier((quarter, payload))
    high, low = call(
        weights_kernel,
        [shape(D, QKV + D, kind=bf16), shape(D, QKV + D, kind=bf16)],
        [],
        (place,),
        *far_weights(own, quarter),
        name="weights",
    )
    tiles = exchange(payload.reshape(FRAMES, CHUNK, 1, 128), "tm")

    times = jnp.tile(frame_times[0].astype(f32), HALF // FRAMES)
    i = lax.broadcasted_iota(jnp.int32, (HALF, HALF), 0)
    j = lax.broadcasted_iota(jnp.int32, (HALF, HALF), 1)
    seen = (i // FRAMES == j // FRAMES) & (j <= i)
    spacing = jnp.where(seen, times[:, None] - times[None, :], f32(1e30))

    grads, tokens_back = call(
        sublayer_kernel,
        [shape(NY * NC, NX, TILES, 8, 128), shape(ROWS * 4, 128)],
        [
            pltpu.VMEM((NY * NC, NX, TILES, 8, 128), f32), pltpu.VMEM((ROWS * 4, 128), f32),
            pltpu.SemaphoreType.DMA((20,)),
            pltpu.VMEM((D, QKV + D), bf16), pltpu.VMEM((D, QKV + D), bf16),
            pltpu.VMEM((ROWS, D), f32), pltpu.VMEM((ROWS, D), f32),
            pltpu.VMEM((ROWS, QKV), bf16), pltpu.VMEM((ROWS, QKV), bf16),
            pltpu.VMEM((ROWS, D), bf16), pltpu.VMEM((ROWS, D), bf16),
            pltpu.VMEM((ROWS, D), f32),
            pltpu.VMEM((ROWS, QKV), bf16), pltpu.VMEM((ROWS, QKV), bf16),
        ],
        (slopes,),
        tiles.reshape(FRAMES * CHUNK, 128), norm_gain.reshape(1, D), spacing, high, low,
        name="sublayer", far_ins=2, far_outs=2, limit=48,
    )
    grad_tokens = exchange(tokens_back.reshape(FRAMES, 4, OWN, 128), "tm")

    row = lax.psum_scatter(
        grads, "dp", scatter_dimension=0, axis_index_groups=YC_GROUPS, tiled=True
    ).reshape(NX, TILES, 8, 128)
    row, grad_tokens = lax.optimization_barrier((row, grad_tokens))
    plane = jnp.sum(exchange(row, "tm", X_GROUPS), axis=0)
    column = jnp.concatenate(
        [
            plane[:32].reshape(16, 16, 1, 128),
            jnp.tile(plane[32:40], (2, 1, 1)).reshape(16, 8, 1, 128),
            jnp.tile(plane[40], (2, 1)).reshape(16, 1, 1, 128),
        ],
        axis=1,
    )
    total = jnp.sum(exchange(column, BOTH, Z_GROUPS), axis=0)

    line = exchange(jnp.broadcast_to(total, (NZL, 25, 1, 128)), "tm", ZL_GROUPS)
    grad_gain = line[:, 24, 0, :64].reshape(D)
    line = line[:, :24].reshape(NZL, 3, 8, 128)
    sheet = exchange(jnp.broadcast_to(line, (NX, NZL, 3, 8, 128)), "tm", X_GROUPS)
    main = sheet[:, :, :2].transpose(0, 3, 1, 2, 4).reshape(32, QKV + D)
    half = sheet[:, :, 2].reshape(NX, 4, 2, 8, 128).transpose(0, 1, 3, 2, 4).reshape(ACTIONS, 256)
    other = lax.ppermute(half, "dp", SWAP_CORE)
    grad_table = jnp.where(
        c == 0, jnp.concatenate([half, other], axis=1), jnp.concatenate([other, half], axis=1)
    )
    return (
        grad_tokens.transpose(0, 2, 1, 3).reshape(1, 1, ROWS, D),
        main[:, :QKV],
        main[:, QKV:],
        grad_table,
        grad_gain,
    )


def solution(mesh):
    return jax.shard_map(
        shards,
        mesh=mesh,
        in_specs=(
            P("dp", "tm", None, None),
            P("dp", "tm"),
            P("dp", None),
            P(),
            P(),
            P("dp", None),
            P("dp", None),
            P(),
            P("dp", "tm", None, None),
        ),
        out_specs=(P("dp", "tm", None, None), P("dp", None), P("dp", None), P(), P()),
        check_vma=False,
    )
```

```python
import functools

import jax
import jax.numpy as jnp
from jax import lax
from jax.experimental import pallas as pl
from jax.experimental.pallas import tpu as pltpu
from jax.sharding import PartitionSpec as P

NX, NZL, NY, NZH, NC = 4, 8, 4, 2, 2
D, QKV, HEADS, HEAD, FRAMES, OWN = 512, 1536, 8, 64, 32, 8
ROWS = FRAMES * OWN
HALF = ROWS // 2
PAIR = 2 * HEAD
ACTIONS = 128
TILES = 41
CHUNK = 65
f32, bf16 = jnp.float32, jnp.bfloat16
BOTH = ("tm", "dp")


def tm_of(x, zl):
    return x * NZL + zl


def dp_of(y, zh, c):
    return (y * NZH + zh) * NC + c


def flat_of(x, zl, y, zh, c):
    return tm_of(x, zl) * (NY * NZH * NC) + dp_of(y, zh, c)


XS, ZLS, YS, ZHS, CS = range(NX), range(NZL), range(NY), range(NZH), range(NC)
X_GROUPS = [[tm_of(x, zl) for x in XS] for zl in ZLS]
ZL_GROUPS = [[tm_of(x, zl) for zl in ZLS] for x in XS]
YC_GROUPS = [[dp_of(y, zh, c) for y in YS for c in CS] for zh in ZHS]
Z_GROUPS = [
    [flat_of(x, zl, y, zh, c) for zh in ZHS for zl in ZLS] for x in XS for y in YS for c in CS
]
SWAP_CORE = [(dp_of(y, zh, c), dp_of(y, zh, 1 - c)) for y in YS for zh in ZHS for c in CS]
SWAP_ZH = [(dp_of(y, zh, c), dp_of(y, 1 - zh, c)) for y in YS for zh in ZHS for c in CS]


def turn_y(step):
    return [(dp_of(y, zh, c), dp_of((y + step) % NY, zh, c)) for y in YS for zh in ZHS for c in CS]


def turn_x(step):
    return [(tm_of(x, zl), tm_of((x + step) % NX, zl)) for x in XS for zl in ZLS]


def exchange(value, axis, groups=None):
    return lax.all_to_all(value, axis, 0, 0, axis_index_groups=groups, tiled=True)


def split(value):
    high = value.astype(bf16)
    return high, (value - high.astype(f32)).astype(bf16)


NN = (((1,), (0,)), ((), ()))
NT = (((1,), (1,)), ((), ()))


def dot(a, b, dims=NN):
    return lax.dot_general(a, b, dims, preferred_element_type=f32)


def dot3(a, b, dims=NN):
    return dot(a[0], b[0], dims) + (dot(a[0], b[1], dims) + dot(a[1], b[0], dims))


def take_rows(tiles, rows, start):
    for p in range(OWN):
        for k in range(4):
            rows[p * FRAMES:(p + 1) * FRAMES, k * 128:(k + 1) * 128] = tiles[
                pl.ds((start + k) * 8 + p, FRAMES, stride=CHUNK), :
            ]


def shares_kernel(place, w_qkv, w_out, mine, quarter):
    mine[:, :QKV] = w_qkv[...]
    mine[:, QKV:] = w_out[...]
    x = pl.multiple_of(place[0] * 8, 8)
    quarter[:, :QKV] = w_qkv[pl.ds(x, 8), :]
    quarter[:, QKV:] = w_out[pl.ds(x, 8), :]


def pass_kernel(value, out):
    out[...] = value[...]


def pack_kernel(action, act_table, video, og, out):
    row = act_table[pl.ds(action[0], 1), :]
    tag = jnp.zeros((1, 128), f32) + action[0].astype(f32)
    for f in range(FRAMES):
        rows = slice(f * OWN, f * OWN + OWN)
        for k in range(D // 128):
            cols = slice(k * 128, k * 128 + 128)
            out[f * CHUNK + k * 8:f * CHUNK + k * 8 + 8, :] = video[rows, cols] + row[:, cols]
            out[f * CHUNK + 32 + k * 8:f * CHUNK + 40 + k * 8, :] = og[rows, cols]
        out[f * CHUNK + 64:f * CHUNK + 65, :] = tag


def weights_kernel(place, own, far_mine, far_other, high, low):
    x, y, zh, c = place[0], place[1], place[2], place[3]
    for y_to in YS:
        for side in CS:
            at = pl.ds(pl.multiple_of(y_to * 128 + zh * 64 + side * 32, 32), 32)
            high[at, :], low[at, :] = split(own[y_to * 2 + side])
        turn_y = lax.rem(y - y_to + NY, NY) * NX
        for x_to in range(0, NX, 2):
            turns = [turn_y + lax.rem(x - x_to - i + NX, NX) for i in range(2)]
            for side, ref in ((c, far_mine), (1 - c, far_other)):
                rows = jnp.concatenate([ref[turn] for turn in turns], axis=0)
                at = y_to * 128 + (1 - zh) * 64 + side * 32 + x_to * 8
                at = pl.ds(pl.multiple_of(at, 16), 16)
                high[at, :], low[at, :] = split(rows)


def sublayer_kernel(
    slopes, tiles, gain, spacing, high_in, low_in,
    grads_out, tokens_out,
    grads, tokens_new, sems, high, low, emb_ref, og, qkv_h, qkv_l, gm_h, gm_l, mixed, gr_h, gr_l,
):
    arrivals = [
        pltpu.make_async_copy(source, target, sems.at[18 + i])
        for i, (source, target) in enumerate(((high_in, high), (low_in, low)))
    ]
    for copy in arrivals:
        copy.start()
    take_rows(tiles, emb_ref, 0)
    take_rows(tiles, og, 4)

    tags = tiles[pl.ds(64, FRAMES, stride=CHUNK), :]
    ids = lax.broadcasted_iota(jnp.int32, (FRAMES, ACTIONS), 1).astype(f32)
    pick = jnp.transpose((tags == ids).astype(f32)).astype(bf16)

    emb = emb_ref[...]
    scale = lax.rsqrt(jnp.mean(emb * emb, axis=1, keepdims=True) + 1e-06)
    normed = emb * gain[...] * scale
    parts = split(normed)
    for copy in arrivals:
        copy.wait()
    for block in range(QKV // 256):
        cols = slice(block * 256, block * 256 + 256)
        value = dot3(parts, (high[:, cols], low[:, cols]))
        if block < D // 256:
            value = value * 0.125
        qkv_h[:, cols], qkv_l[:, cols] = split(value)
    og_parts = split(og[...])
    gm_h[...], gm_l[...] = split(dot3(og_parts, (high[:, QKV:], low[:, QKV:]), NT))

    lane = lax.broadcasted_iota(jnp.int32, (ROWS, PAIR), 1) < HEAD
    upper = lax.broadcasted_iota(jnp.int32, (ROWS, PAIR), 0) < HALF
    own_half = lane == upper
    first = lane[:HALF]
    zero = jnp.zeros((ROWS, PAIR), bf16)

    def both_heads(parts):
        twice = [jnp.where(own_half, jnp.concatenate([v, v], axis=0), zero) for v in parts]
        return jnp.concatenate([twice[0], twice[1], twice[0]], axis=1)

    def wide(parts):
        return jnp.concatenate([parts[0], parts[0], parts[1]], axis=1)

    def tall(parts):
        return jnp.concatenate([parts[0], parts[0], parts[1]], axis=0)

    def left(value):
        high_part, low_part = split(value)
        return jnp.concatenate([high_part, low_part, high_part], axis=1)

    def turned(value):
        return jnp.concatenate([jnp.transpose(value[:HALF]), jnp.transpose(value[HALF:])], axis=0)

    def pick_lanes(value):
        return jnp.where(first, value[:HALF], value[HALF:])

    for pair in range(HEADS // 2):
        slope = jnp.concatenate(
            [slopes[pair * 2] * spacing[...], slopes[pair * 2 + 1] * spacing[...]], axis=0
        )
        at = [slice(kind * D + pair * PAIR, kind * D + (pair + 1) * PAIR) for kind in range(3)]
        for g in range(2):
            rows = slice(g * HALF, g * HALF + HALF)
            q, k, v = [(qkv_h[rows, cols], qkv_l[rows, cols]) for cols in at]
            gmp = (gm_h[rows, at[0]], gm_l[rows, at[0]])
            scores = dot(both_heads(q), wide(k), NT) - slope
            raised = jnp.exp(scores - jnp.max(scores, axis=1, keepdims=True))
            weights = raised * (1.0 / jnp.sum(raised, axis=1, keepdims=True))
            d_w = dot(both_heads(gmp), wide(v), NT)
            ds = weights * (d_w - jnp.sum(d_w * weights, axis=1, keepdims=True))
            mixed[rows, at[0]] = pick_lanes(dot(left(weights), tall(v)))
            dq = pick_lanes(dot(left(ds), tall(k))) * 0.125
            dk = pick_lanes(dot(left(turned(ds)), tall(q)))
            dv = pick_lanes(dot(left(turned(weights)), tall(gmp)))
            for cols, value in zip(at, (dq, dk, dv)):
                gr_h[rows, cols], gr_l[rows, cols] = split(value)

    def copy_tiles(tile, count, index):
        part = (slice(None), slice(None), pl.ds(tile, count))
        return pltpu.make_async_copy(grads.at[part], grads_out.at[part], sems.at[index])

    copies = []

    def send_tiles(tile, count, index):
        copies.append(copy_tiles(tile, count, index))
        copies[-1].start()

    def place_columns(block, value):
        for y in YS:
            for side in CS:
                for x in XS:
                    for zh in ZHS:
                        r = y * 128 + zh * 64 + side * 32 + x * 8
                        for half in range(2):
                            grads[y * 2 + side, x, (zh * 8 + block) * 2 + half] = value[
                                r:r + 8, half * 128:half * 128 + 128
                            ]
        for zh in ZHS:
            send_tiles((zh * 8 + block) * 2, 2, block * 2 + zh)

    normt = split(jnp.transpose(normed))
    for block in range(QKV // 256):
        cols = slice(block * 256, block * 256 + 256)
        place_columns(block, dot3(normt, (gr_h[:, cols], gr_l[:, cols])))
    mixt = split(jnp.transpose(mixed[...]))
    for block in range(2):
        cols = slice(block * 256, block * 256 + 256)
        place_columns(6 + block, dot3(mixt, (og_parts[0][:, cols], og_parts[1][:, cols])))

    gn = dot3((gr_h[...], gr_l[...]), (high[:, :QKV], low[:, :QKV]), NT)
    gain_sum = jnp.sum(gn * emb * scale, axis=0, keepdims=True)
    u = gn * gain[...]
    along = jnp.sum(u * emb, axis=1, keepdims=True) * (scale * scale * scale) * (1.0 / D)
    tokens = og[...] + (u * scale - emb * along)
    total = jnp.zeros((FRAMES, D), f32)
    for p in range(OWN):
        piece = tokens[p * FRAMES:(p + 1) * FRAMES, :]
        for k in range(4):
            tokens_new[pl.ds(k * 8 + p, FRAMES, stride=32), :] = piece[:, k * 128:(k + 1) * 128]
        total = total + piece
    copies.append(pltpu.make_async_copy(tokens_new, tokens_out, sems.at[17]))
    copies[-1].start()
    total_h, total_l = split(total)
    table = dot(pick, total_h) + dot(pick, total_l)
    gain_tile = jnp.concatenate(
        [gain_sum[:, i * 64:(i + 1) * 64] for i in range(8)], axis=0
    )
    gain_tile = jnp.concatenate([gain_tile, jnp.zeros((8, 64), f32)], axis=1
    )
    for x in XS:
        for side in CS:
            for k in range(8):
                r, start = x * 32 + (k // 2) * 8, side * 256 + (k % 2) * 128
                for y in YS:
                    grads[y * 2 + side, x, 32 + k] = table[r:r + 8, start:start + 128]
            for y in YS:
                grads[y * 2 + side, x, 40] = gain_tile
    send_tiles(32, 9, 16)
    for copy in copies:
        copy.wait()


def call(kernel, outs, scratch, scalars, *arrays, name, far_ins=0, far_outs=0, limit=60, work=None):
    vmem = pl.BlockSpec(memory_space=pltpu.VMEM)
    smem = pl.BlockSpec(memory_space=pltpu.SMEM)
    hbm = pl.BlockSpec(memory_space=pltpu.HBM)
    return pl.pallas_call(
        kernel,
        out_shape=outs,
        in_specs=[smem] * len(scalars) + [vmem] * (len(arrays) - far_ins) + [hbm] * far_ins,
        out_specs=[hbm] * far_outs + [vmem] * (len(outs) - far_outs),
        scratch_shapes=scratch,
        compiler_params=pltpu.CompilerParams(vmem_limit_bytes=limit * 1024 * 1024),
        cost_estimate=work
        and pl.CostEstimate(flops=work, bytes_accessed=0, transcendentals=0),
        name=name,
    )(*scalars, *arrays)


def shape(*dims, kind=f32):
    return jax.ShapeDtypeStruct(dims, kind)


def far_weights(own, quarter):
    row = jnp.stack([quarter] + [lax.ppermute(quarter, "tm", turn_x(i)) for i in range(1, NX)])
    row, own = lax.optimization_barrier((row, own))
    far = jnp.concatenate([row] + [lax.ppermute(row, "dp", turn_y(i)) for i in range(1, NY)])
    return own, far, lax.ppermute(far, "dp", SWAP_CORE)


def shards(
    video_tokens, actions, frame_times, act_table, norm_gain, w_qkv, w_out, slopes, out_grad
):
    t, d = lax.axis_index("tm"), lax.axis_index("dp")
    x, y, zh, c = t // NZL, d // (NZH * NC), (d // NC) % NZH, d % NC
    place = jnp.stack([x, y, zh, c]).astype(jnp.int32)

    mine, quarter = call(
        shares_kernel,
        [shape(32, QKV + D), shape(8, QKV + D)],
        [],
        (place,),
        w_qkv, w_out,
        name="shares",
    )
    own = lax.all_gather(mine, "dp", axis_index_groups=YC_GROUPS)
    quarter = lax.ppermute(quarter, "dp", SWAP_ZH)
    quarter = call(
        pass_kernel, [shape(8, QKV + D)], [], (), quarter, name="swapped", work=20000000000
    )[0]
    payload = call(
        pack_kernel,
        [shape(FRAMES * CHUNK, 128)],
        [],
        (actions.reshape(1),),
        act_table, video_tokens[0, 0], out_grad[0, 0],
        name="pack",
    )[0]
    high, low = call(
        weights_kernel,
        [shape(D, QKV + D, kind=bf16), shape(D, QKV + D, kind=bf16)],
        [],
        (place,),
        *far_weights(own, quarter),
        name="weights",
    )
    tiles = exchange(payload.reshape(FRAMES, CHUNK, 1, 128), "tm")

    times = jnp.tile(frame_times[0].astype(f32), HALF // FRAMES)
    i = lax.broadcasted_iota(jnp.int32, (HALF, HALF), 0)
    j = lax.broadcasted_iota(jnp.int32, (HALF, HALF), 1)
    seen = (i // FRAMES == j // FRAMES) & (j <= i)
    spacing = jnp.where(seen, times[:, None] - times[None, :], f32(1e30))

    grads, tokens_back = call(
        sublayer_kernel,
        [shape(NY * NC, NX, TILES, 8, 128), shape(ROWS * 4, 128)],
        [
            pltpu.VMEM((NY * NC, NX, TILES, 8, 128), f32), pltpu.VMEM((ROWS * 4, 128), f32),
            pltpu.SemaphoreType.DMA((20,)),
            pltpu.VMEM((D, QKV + D), bf16), pltpu.VMEM((D, QKV + D), bf16),
            pltpu.VMEM((ROWS, D), f32), pltpu.VMEM((ROWS, D), f32),
            pltpu.VMEM((ROWS, QKV), bf16), pltpu.VMEM((ROWS, QKV), bf16),
            pltpu.VMEM((ROWS, D), bf16), pltpu.VMEM((ROWS, D), bf16),
            pltpu.VMEM((ROWS, D), f32),
            pltpu.VMEM((ROWS, QKV), bf16), pltpu.VMEM((ROWS, QKV), bf16),
        ],
        (slopes,),
        tiles.reshape(FRAMES * CHUNK, 128), norm_gain.reshape(1, D), spacing, high, low,
        name="sublayer", far_ins=2, far_outs=2, limit=52,
    )
    grad_tokens = exchange(tokens_back.reshape(FRAMES, 4, OWN, 128), "tm")

    row = lax.psum_scatter(
        grads, "dp", scatter_dimension=0, axis_index_groups=YC_GROUPS, tiled=True
    ).reshape(NX, TILES, 8, 128)
    row, grad_tokens = lax.optimization_barrier((row, grad_tokens))
    plane = jnp.sum(exchange(row, "tm", X_GROUPS), axis=0)
    column = jnp.concatenate(
        [
            plane[:32].reshape(16, 16, 1, 128),
            jnp.tile(plane[32:40], (2, 1, 1)).reshape(16, 8, 1, 128),
            jnp.tile(plane[40], (2, 1)).reshape(16, 1, 1, 128),
        ],
        axis=1,
    )
    total = jnp.sum(exchange(column, BOTH, Z_GROUPS), axis=0)

    line = exchange(jnp.broadcast_to(total, (NZL, 25, 1, 128)), "tm", ZL_GROUPS)
    grad_gain = line[:, 24, 0, :64].reshape(D)
    line = line[:, :24].reshape(NZL, 3, 8, 128)
    sheet = exchange(jnp.broadcast_to(line, (NX, NZL, 3, 8, 128)), "tm", X_GROUPS)
    main = sheet[:, :, :2].transpose(0, 3, 1, 2, 4).reshape(32, QKV + D)
    half = sheet[:, :, 2].reshape(NX, 4, 2, 8, 128).transpose(0, 1, 3, 2, 4).reshape(ACTIONS, 256)
    other = lax.ppermute(half, "dp", SWAP_CORE)
    grad_table = jnp.where(
        c == 0, jnp.concatenate([half, other], axis=1), jnp.concatenate([other, half], axis=1)
    )
    return (
        grad_tokens.transpose(0, 2, 1, 3).reshape(1, 1, ROWS, D),
        main[:, :QKV],
        main[:, QKV:],
        grad_table,
        grad_gain,
    )


def solution(mesh):
    return jax.shard_map(
        shards,
        mesh=mesh,
        in_specs=(
            P("dp", "tm", None, None),
            P("dp", "tm"),
            P("dp", None),
            P(),
            P(),
            P("dp", None),
            P("dp", None),
            P(),
            P("dp", "tm", None, None),
        ),
        out_specs=(P("dp", "tm", None, None), P("dp", None), P("dp", None), P(), P()),
        check_vma=False,
    )
```

```python
import functools

import jax
import jax.numpy as jnp
from jax import lax
from jax.experimental import pallas as pl
from jax.experimental.pallas import tpu as pltpu
from jax.sharding import PartitionSpec as P

NX, NZL, NY, NZH, NC = 4, 8, 4, 2, 2
D, QKV, HEADS, HEAD, FRAMES, OWN = 512, 1536, 8, 64, 32, 8
ROWS = FRAMES * OWN
HALF = ROWS // 2
PAIR = 2 * HEAD
ACTIONS = 128
TILES = 32
CHUNK = 65
f32, bf16 = jnp.float32, jnp.bfloat16
BOTH = ("tm", "dp")


def tm_of(x, zl):
    return x * NZL + zl


def dp_of(y, zh, c):
    return (y * NZH + zh) * NC + c


def flat_of(x, zl, y, zh, c):
    return tm_of(x, zl) * (NY * NZH * NC) + dp_of(y, zh, c)


XS, ZLS, YS, ZHS, CS = range(NX), range(NZL), range(NY), range(NZH), range(NC)
X_GROUPS = [[tm_of(x, zl) for x in XS] for zl in ZLS]
ZL_GROUPS = [[tm_of(x, zl) for zl in ZLS] for x in XS]
YC_GROUPS = [[dp_of(y, zh, c) for y in YS for c in CS] for zh in ZHS]
Z_GROUPS = [
    [flat_of(x, zl, y, zh, c) for zh in ZHS for zl in ZLS] for x in XS for y in YS for c in CS
]
SWAP_CORE = [(dp_of(y, zh, c), dp_of(y, zh, 1 - c)) for y in YS for zh in ZHS for c in CS]
SWAP_ZH = [(dp_of(y, zh, c), dp_of(y, 1 - zh, c)) for y in YS for zh in ZHS for c in CS]


def turn_y(step):
    return [(dp_of(y, zh, c), dp_of((y + step) % NY, zh, c)) for y in YS for zh in ZHS for c in CS]


def swap_y(bit):
    return [(dp_of(y, zh, c), dp_of(y ^ bit, zh, c)) for y in YS for zh in ZHS for c in CS]


def turn_x(step):
    return [(tm_of(x, zl), tm_of((x + step) % NX, zl)) for x in XS for zl in ZLS]


def exchange(value, axis, groups=None):
    return lax.all_to_all(value, axis, 0, 0, axis_index_groups=groups, tiled=True)


def split(value):
    high = value.astype(bf16)
    return high, (value - high.astype(f32)).astype(bf16)


NN = (((1,), (0,)), ((), ()))
NT = (((1,), (1,)), ((), ()))


def dot(a, b, dims=NN):
    return lax.dot_general(a, b, dims, preferred_element_type=f32)


def dot3(a, b, dims=NN):
    return dot(a[0], b[0], dims) + (dot(a[0], b[1], dims) + dot(a[1], b[0], dims))


def take_rows(tiles, rows, start):
    for p in range(OWN):
        for k in range(4):
            rows[p * FRAMES:(p + 1) * FRAMES, k * 128:(k + 1) * 128] = tiles[
                pl.ds((start + k) * 8 + p, FRAMES, stride=CHUNK), :
            ]


def shares_kernel(place, w_qkv, w_out, mine, quarter):
    mine[:, :QKV] = w_qkv[...]
    mine[:, QKV:] = w_out[...]
    x = pl.multiple_of(place[0] * 8, 8)
    quarter[:, :QKV] = w_qkv[pl.ds(x, 8), :]
    quarter[:, QKV:] = w_out[pl.ds(x, 8), :]


def pass_kernel(value, out):
    out[...] = value[...]


def pack_kernel(action, act_table, video, og, out):
    row = act_table[pl.ds(action[0], 1), :]
    tag = jnp.zeros((1, 128), f32) + action[0].astype(f32)
    for f in range(FRAMES):
        rows = slice(f * OWN, f * OWN + OWN)
        for k in range(D // 128):
            cols = slice(k * 128, k * 128 + 128)
            out[f * CHUNK + k * 8:f * CHUNK + k * 8 + 8, :] = video[rows, cols] + row[:, cols]
            out[f * CHUNK + 32 + k * 8:f * CHUNK + 40 + k * 8, :] = og[rows, cols]
        out[f * CHUNK + 64:f * CHUNK + 65, :] = tag


def unpack_kernel(tiles, out):
    for f in range(FRAMES):
        for k in range(D // 128):
            out[f * OWN:f * OWN + OWN, k * 128:k * 128 + 128] = tiles[f, k]


def weights_kernel(place, own, far_mine, far_other, high, low):
    x, y, zh, c = place[0], place[1], place[2], place[3]
    for y_to in YS:
        for side in CS:
            at = pl.ds(pl.multiple_of(y_to * 128 + zh * 64 + side * 32, 32), 32)
            high[at, :], low[at, :] = split(own[y_to * 2 + side])
        turn_y = lax.rem(y - y_to + NY, NY) * NX
        for x_to in range(0, NX, 2):
            turns = [turn_y + lax.rem(x - x_to - i + NX, NX) for i in range(2)]
            for side, ref in ((c, far_mine), (1 - c, far_other)):
                rows = jnp.concatenate([ref[turn] for turn in turns], axis=0)
                at = y_to * 128 + (1 - zh) * 64 + side * 32 + x_to * 8
                at = pl.ds(pl.multiple_of(at, 16), 16)
                high[at, :], low[at, :] = split(rows)


def sublayer_kernel(
    tiles, extras_in, high_in, low_in,
    grads_out, tokens_out, tables,
    grads, tokens_new, sems, extras, high, low, emb_ref, og, qkv_h, qkv_l, gm_h, gm_l, mixed, gr_h, gr_l,
):
    arrivals = [
        pltpu.make_async_copy(source, target, sems.at[17 + i])
        for i, (source, target) in enumerate(
            ((extras_in, extras), (high_in, high), (low_in, low))
        )
    ]
    for copy in arrivals:
        copy.start()
    take_rows(tiles, emb_ref, 0)
    take_rows(tiles, og, 4)

    tags = tiles[pl.ds(64, FRAMES, stride=CHUNK), :]
    ids = lax.broadcasted_iota(jnp.int32, (FRAMES, ACTIONS), 1).astype(f32)
    pick = jnp.transpose((tags == ids).astype(f32)).astype(bf16)

    emb = emb_ref[...]
    scale = lax.rsqrt(jnp.mean(emb * emb, axis=1, keepdims=True) + 1e-06)
    arrivals[0].wait()
    spacing = extras[:HALF, :]
    gain = jnp.concatenate([extras[HALF + HEADS + i:HALF + HEADS + i + 1, :] for i in range(4)], axis=1)
    normed = emb * gain * scale
    parts = split(normed)
    for copy in arrivals[1:]:
        copy.wait()
    for block in range(QKV // 256):
        cols = slice(block * 256, block * 256 + 256)
        value = dot3(parts, (high[:, cols], low[:, cols]))
        if block < D // 256:
            value = value * 0.125
        qkv_h[:, cols], qkv_l[:, cols] = split(value)
    og_parts = split(og[...])
    gm_h[...], gm_l[...] = split(dot3(og_parts, (high[:, QKV:], low[:, QKV:]), NT))

    lane = lax.broadcasted_iota(jnp.int32, (ROWS, PAIR), 1) < HEAD
    upper = lax.broadcasted_iota(jnp.int32, (ROWS, PAIR), 0) < HALF
    own_half = lane == upper
    first = lane[:HALF]
    zero = jnp.zeros((ROWS, PAIR), bf16)

    def both_heads(parts):
        twice = [jnp.where(own_half, jnp.concatenate([v, v], axis=0), zero) for v in parts]
        return jnp.concatenate([twice[0], twice[1], twice[0]], axis=1)

    def wide(parts):
        return jnp.concatenate([parts[0], parts[0], parts[1]], axis=1)

    def tall(parts):
        return jnp.concatenate([parts[0], parts[0], parts[1]], axis=0)

    def left(value):
        high_part, low_part = split(value)
        return jnp.concatenate([high_part, low_part, high_part], axis=1)

    def turned(value):
        return jnp.concatenate([jnp.transpose(value[:HALF]), jnp.transpose(value[HALF:])], axis=0)

    def pick_lanes(value):
        return jnp.where(first, value[:HALF], value[HALF:])

    for pair in range(HEADS // 2):
        slope = jnp.concatenate(
            [extras[HALF + pair * 2 + i:HALF + pair * 2 + i + 1, :] * spacing for i in range(2)], axis=0
        )
        at = [slice(kind * D + pair * PAIR, kind * D + (pair + 1) * PAIR) for kind in range(3)]
        for g in range(2):
            rows = slice(g * HALF, g * HALF + HALF)
            q, k, v = [(qkv_h[rows, cols], qkv_l[rows, cols]) for cols in at]
            gmp = (gm_h[rows, at[0]], gm_l[rows, at[0]])
            scores = dot(both_heads(q), wide(k), NT) - slope
            raised = jnp.exp(scores - jnp.max(scores, axis=1, keepdims=True))
            weights = raised * (1.0 / jnp.sum(raised, axis=1, keepdims=True))
            d_w = dot(both_heads(gmp), wide(v), NT)
            ds = weights * (d_w - jnp.sum(d_w * weights, axis=1, keepdims=True))
            mixed[rows, at[0]] = pick_lanes(dot(left(weights), tall(v)))
            dq = pick_lanes(dot(left(ds), tall(k))) * 0.125
            dk = pick_lanes(dot(left(turned(ds)), tall(q)))
            dv = pick_lanes(dot(left(turned(weights)), tall(gmp)))
            for cols, value in zip(at, (dq, dk, dv)):
                gr_h[rows, cols], gr_l[rows, cols] = split(value)

    def copy_tiles(tile, count, index):
        part = (slice(None), slice(None), pl.ds(tile, count))
        return pltpu.make_async_copy(grads.at[part], grads_out.at[part], sems.at[index])

    copies = []

    def send_tiles(tile, count, index):
        copies.append(copy_tiles(tile, count, index))
        copies[-1].start()

    def place_columns(block, value):
        for y in YS:
            for side in CS:
                for x in XS:
                    for zh in ZHS:
                        r = y * 128 + zh * 64 + side * 32 + x * 8
                        for half in range(2):
                            grads[y * 2 + side, x, (zh * 8 + block) * 2 + half] = value[
                                r:r + 8, half * 128:half * 128 + 128
                            ]
        for zh in ZHS:
            send_tiles((zh * 8 + block) * 2, 2, block * 2 + zh)

    gn = dot3((gr_h[...], gr_l[...]), (high[:, :QKV], low[:, :QKV]), NT)
    gain_sum = jnp.sum(gn * emb * scale, axis=0, keepdims=True)
    u = gn * gain
    along = jnp.sum(u * emb, axis=1, keepdims=True) * (scale * scale * scale) * (1.0 / D)
    tokens = og[...] + (u * scale - emb * along)
    total = jnp.zeros((FRAMES, D), f32)
    for p in range(OWN):
        piece = tokens[p * FRAMES:(p + 1) * FRAMES, :]
        for k in range(4):
            tokens_new[pl.ds(k * 8 + p, FRAMES, stride=32), :] = piece[:, k * 128:(k + 1) * 128]
        total = total + piece
    copies.append(pltpu.make_async_copy(tokens_new, tokens_out, sems.at[16]))
    copies[-1].start()
    total_h, total_l = split(total)
    table = dot(pick, total_h) + dot(pick, total_l)
    gain_tile = jnp.concatenate(
        [gain_sum[:, i * 64:(i + 1) * 64] for i in range(8)], axis=0
    )
    gain_tile = jnp.concatenate([gain_tile, jnp.zeros((8, 64), f32)], axis=1
    )
    for x in XS:
        for side in CS:
            for k in range(8):
                r, start = x * 32 + (k // 2) * 8, side * 256 + (k % 2) * 128
                tables[side, x, k] = table[r:r + 8, start:start + 128]
            tables[side, x, 8] = gain_tile
    normt = split(jnp.transpose(normed))
    for block in range(QKV // 256):
        cols = slice(block * 256, block * 256 + 256)
        place_columns(block, dot3(normt, (gr_h[:, cols], gr_l[:, cols])))
    mixt = split(jnp.transpose(mixed[...]))
    for block in range(2):
        cols = slice(block * 256, block * 256 + 256)
        place_columns(6 + block, dot3(mixt, (og_parts[0][:, cols], og_parts[1][:, cols])))
    for copy in copies:
        copy.wait()


def call(kernel, outs, scratch, scalars, *arrays, name, far_ins=0, far_outs=0, limit=60, work=None):
    vmem = pl.BlockSpec(memory_space=pltpu.VMEM)
    smem = pl.BlockSpec(memory_space=pltpu.SMEM)
    hbm = pl.BlockSpec(memory_space=pltpu.HBM)
    return pl.pallas_call(
        kernel,
        out_shape=outs,
        in_specs=[smem] * len(scalars) + [vmem] * (len(arrays) - far_ins) + [hbm] * far_ins,
        out_specs=[hbm] * far_outs + [vmem] * (len(outs) - far_outs),
        scratch_shapes=scratch,
        compiler_params=pltpu.CompilerParams(vmem_limit_bytes=limit * 1024 * 1024),
        cost_estimate=work
        and pl.CostEstimate(flops=work, bytes_accessed=0, transcendentals=0),
        name=name,
    )(*scalars, *arrays)


def shape(*dims, kind=f32):
    return jax.ShapeDtypeStruct(dims, kind)


def far_weights(own, quarter):
    row = jnp.stack([quarter] + [lax.ppermute(quarter, "tm", turn_x(i)) for i in range(1, NX)])
    row, own = lax.optimization_barrier((row, own))
    far = jnp.concatenate([row] + [lax.ppermute(row, "dp", turn_y(i)) for i in range(1, NY)])
    return own, far, lax.ppermute(far, "dp", SWAP_CORE)


def shards(
    video_tokens, actions, frame_times, act_table, norm_gain, w_qkv, w_out, slopes, out_grad
):
    t, d = lax.axis_index("tm"), lax.axis_index("dp")
    x, y, zh, c = t // NZL, d // (NZH * NC), (d // NC) % NZH, d % NC
    place = jnp.stack([x, y, zh, c]).astype(jnp.int32)

    mine, quarter = call(
        shares_kernel,
        [shape(32, QKV + D), shape(8, QKV + D)],
        [],
        (place,),
        w_qkv, w_out,
        name="shares",
    )
    own = lax.all_gather(mine, "dp", axis_index_groups=YC_GROUPS)
    quarter = lax.ppermute(quarter, "dp", SWAP_ZH)
    quarter = call(
        pass_kernel, [shape(8, QKV + D)], [], (), quarter, name="swapped", work=20000000000
    )[0]
    payload = call(
        pack_kernel,
        [shape(FRAMES * CHUNK, 128)],
        [],
        (actions.reshape(1),),
        act_table, video_tokens[0, 0], out_grad[0, 0],
        name="pack",
    )[0]
    high, low = call(
        weights_kernel,
        [shape(D, QKV + D, kind=bf16), shape(D, QKV + D, kind=bf16)],
        [],
        (place,),
        *far_weights(own, quarter),
        name="weights",
    )
    tiles = exchange(payload.reshape(FRAMES, CHUNK, 1, 128), "tm")

    times = jnp.tile(frame_times[0].astype(f32), HALF // FRAMES)
    i = lax.broadcasted_iota(jnp.int32, (HALF, HALF), 0)
    j = lax.broadcasted_iota(jnp.int32, (HALF, HALF), 1)
    seen = (i // FRAMES == j // FRAMES) & (j <= i)
    spacing = jnp.where(seen, times[:, None] - times[None, :], f32(1e30))
    extras = jnp.concatenate(
        [
            spacing, jnp.broadcast_to(slopes[:, None], (HEADS, 128)),
            norm_gain.reshape(4, 128), jnp.zeros((4, 128), f32),
        ]
    )

    grads, tokens_back, tables = call(
        sublayer_kernel,
        [
            shape(NY * NC, NX, TILES, 8, 128), shape(ROWS * 4, 128),
            shape(NC, NX, 9, 8, 128),
        ],
        [
            pltpu.VMEM((NY * NC, NX, TILES, 8, 128), f32), pltpu.VMEM((ROWS * 4, 128), f32),
            pltpu.SemaphoreType.DMA((20,)), pltpu.VMEM((HALF + 16, 128), f32),
            pltpu.VMEM((D, QKV + D), bf16), pltpu.VMEM((D, QKV + D), bf16),
            pltpu.VMEM((ROWS, D), f32), pltpu.VMEM((ROWS, D), f32),
            pltpu.VMEM((ROWS, QKV), bf16), pltpu.VMEM((ROWS, QKV), bf16),
            pltpu.VMEM((ROWS, D), bf16), pltpu.VMEM((ROWS, D), bf16),
            pltpu.VMEM((ROWS, D), f32),
            pltpu.VMEM((ROWS, QKV), bf16), pltpu.VMEM((ROWS, QKV), bf16),
        ],
        (),
        tiles.reshape(FRAMES * CHUNK, 128), extras, high, low,
        name="sublayer", far_ins=3, far_outs=2, limit=52,
    )
    tokens_there = exchange(tokens_back.reshape(FRAMES, 4, OWN, 128), "tm")

    row = lax.psum_scatter(
        grads, "dp", scatter_dimension=0, axis_index_groups=YC_GROUPS, tiled=True
    ).reshape(NX, TILES, 8, 128)
    part = lax.dynamic_index_in_dim(tables, c, 0, False) + lax.ppermute(
        lax.dynamic_index_in_dim(tables, 1 - c, 0, False), "dp", SWAP_CORE
    )
    for bit in (1, 2):
        part = part + lax.ppermute(part, "dp", swap_y(bit))
    part, tokens_there = lax.optimization_barrier((part, tokens_there))
    part = jnp.sum(exchange(part, "tm", X_GROUPS), axis=0)
    grad_tokens = call(
        unpack_kernel, [shape(ROWS, D)], [], (), tokens_there, name="unpack"
    )[0]
    row, part, grad_tokens = lax.optimization_barrier((row, part, grad_tokens))
    plane = jnp.sum(exchange(row, "tm", X_GROUPS), axis=0)
    column = jnp.concatenate(
        [
            plane.reshape(16, 16, 1, 128),
            jnp.tile(part[:8], (2, 1, 1)).reshape(16, 8, 1, 128),
            jnp.tile(part[8], (2, 1)).reshape(16, 1, 1, 128),
        ],
        axis=1,
    )
    total = jnp.sum(exchange(column, BOTH, Z_GROUPS), axis=0)

    line = exchange(jnp.broadcast_to(total, (NZL, 25, 1, 128)), "tm", ZL_GROUPS)
    grad_gain = line[:, 24, 0, :64].reshape(D)
    line = line[:, :24].reshape(NZL, 3, 8, 128)
    sheet = exchange(jnp.broadcast_to(line, (NX, NZL, 3, 8, 128)), "tm", X_GROUPS)
    main = sheet[:, :, :2].transpose(0, 3, 1, 2, 4).reshape(32, QKV + D)
    half = sheet[:, :, 2].reshape(NX, 4, 2, 8, 128).transpose(0, 1, 3, 2, 4).reshape(ACTIONS, 256)
    other = lax.ppermute(half, "dp", SWAP_CORE)
    grad_table = jnp.where(
        c == 0, jnp.concatenate([half, other], axis=1), jnp.concatenate([other, half], axis=1)
    )
    return (
        grad_tokens.reshape(1, 1, ROWS, D),
        main[:, :QKV],
        main[:, QKV:],
        grad_table,
        grad_gain,
    )


def solution(mesh):
    return jax.shard_map(
        shards,
        mesh=mesh,
        in_specs=(
            P("dp", "tm", None, None),
            P("dp", "tm"),
            P("dp", None),
            P(),
            P(),
            P("dp", None),
            P("dp", None),
            P(),
            P("dp", "tm", None, None),
        ),
        out_specs=(P("dp", "tm", None, None), P("dp", None), P("dp", None), P(), P()),
        check_vma=False,
    )
```

```python
import functools

import jax
import jax.numpy as jnp
from jax import lax
from jax.experimental import pallas as pl
from jax.experimental.pallas import tpu as pltpu
from jax.sharding import PartitionSpec as P

NX, NZL, NY, NZH, NC = 4, 8, 4, 2, 2
D, QKV, HEADS, HEAD, FRAMES, OWN = 512, 1536, 8, 64, 32, 8
ROWS = FRAMES * OWN
HALF = ROWS // 2
PAIR = 2 * HEAD
ACTIONS = 128
TILES = 32
CHUNK = 65
f32, bf16 = jnp.float32, jnp.bfloat16
BOTH = ("tm", "dp")


def tm_of(x, zl):
    return x * NZL + zl


def dp_of(y, zh, c):
    return (y * NZH + zh) * NC + c


def flat_of(x, zl, y, zh, c):
    return tm_of(x, zl) * (NY * NZH * NC) + dp_of(y, zh, c)


XS, ZLS, YS, ZHS, CS = range(NX), range(NZL), range(NY), range(NZH), range(NC)
X_GROUPS = [[tm_of(x, zl) for x in XS] for zl in ZLS]
ZL_GROUPS = [[tm_of(x, zl) for zl in ZLS] for x in XS]
YC_GROUPS = [[dp_of(y, zh, c) for y in YS for c in CS] for zh in ZHS]
Z_GROUPS = [
    [flat_of(x, zl, y, zh, c) for zh in ZHS for zl in ZLS] for x in XS for y in YS for c in CS
]
SWAP_CORE = [(dp_of(y, zh, c), dp_of(y, zh, 1 - c)) for y in YS for zh in ZHS for c in CS]
SWAP_ZH = [(dp_of(y, zh, c), dp_of(y, 1 - zh, c)) for y in YS for zh in ZHS for c in CS]


def turn_y(step):
    return [(dp_of(y, zh, c), dp_of((y + step) % NY, zh, c)) for y in YS for zh in ZHS for c in CS]


def swap_y(bit):
    return [(dp_of(y, zh, c), dp_of(y ^ bit, zh, c)) for y in YS for zh in ZHS for c in CS]


def turn_x(step):
    return [(tm_of(x, zl), tm_of((x + step) % NX, zl)) for x in XS for zl in ZLS]


def exchange(value, axis, groups=None):
    return lax.all_to_all(value, axis, 0, 0, axis_index_groups=groups, tiled=True)


def split(value):
    high = value.astype(bf16)
    return high, (value - high.astype(f32)).astype(bf16)


NN = (((1,), (0,)), ((), ()))
NT = (((1,), (1,)), ((), ()))


def dot(a, b, dims=NN):
    return lax.dot_general(a, b, dims, preferred_element_type=f32)


def dot3(a, b, dims=NN):
    return dot(a[0], b[0], dims) + (dot(a[0], b[1], dims) + dot(a[1], b[0], dims))


def take_rows(tiles, rows, start):
    for p in range(OWN):
        for k in range(4):
            rows[p * FRAMES:(p + 1) * FRAMES, k * 128:(k + 1) * 128] = tiles[
                pl.ds((start + k) * 8 + p, FRAMES, stride=CHUNK), :
            ]


def pass_kernel(value, out):
    out[...] = value[...]


def front_kernel(place, action, act_table, video, og, w_qkv, w_out, out, mine, quarter):
    mine[:, :QKV] = w_qkv[...]
    mine[:, QKV:] = w_out[...]
    x = pl.multiple_of(place[0] * 8, 8)
    quarter[:, :QKV] = w_qkv[pl.ds(x, 8), :]
    quarter[:, QKV:] = w_out[pl.ds(x, 8), :]
    row = act_table[pl.ds(action[0], 1), :]
    tag = jnp.zeros((1, 128), f32) + action[0].astype(f32)
    for f in range(FRAMES):
        rows = slice(f * OWN, f * OWN + OWN)
        for k in range(D // 128):
            cols = slice(k * 128, k * 128 + 128)
            out[f * CHUNK + k * 8:f * CHUNK + k * 8 + 8, :] = video[rows, cols] + row[:, cols]
            out[f * CHUNK + 32 + k * 8:f * CHUNK + 40 + k * 8, :] = og[rows, cols]
        out[f * CHUNK + 64:f * CHUNK + 65, :] = tag


def unpack_kernel(tiles, out):
    for f in range(FRAMES):
        for k in range(D // 128):
            out[f * OWN:f * OWN + OWN, k * 128:k * 128 + 128] = tiles[f, k]


def weights_kernel(place, own, far_mine, far_other, high, low):
    x, y, zh, c = place[0], place[1], place[2], place[3]
    for y_to in YS:
        for side in CS:
            at = pl.ds(pl.multiple_of(y_to * 128 + zh * 64 + side * 32, 32), 32)
            high[at, :], low[at, :] = split(own[y_to * 2 + side])
        turn_y = lax.rem(y - y_to + NY, NY) * NX
        for x_to in range(0, NX, 2):
            turns = [turn_y + lax.rem(x - x_to - i + NX, NX) for i in range(2)]
            for side, ref in ((c, far_mine), (1 - c, far_other)):
                rows = jnp.concatenate([ref[turn] for turn in turns], axis=0)
                at = y_to * 128 + (1 - zh) * 64 + side * 32 + x_to * 8
                at = pl.ds(pl.multiple_of(at, 16), 16)
                high[at, :], low[at, :] = split(rows)


def sublayer_kernel(
    tiles, extras_in, high_in, low_in,
    grads_out, tokens_out, tables,
    grads, tokens_new, sems, extras, high, low, emb_ref, og, qkv_h, qkv_l, gm_h, gm_l, mixed, gr_h, gr_l,
):
    arrivals = [
        pltpu.make_async_copy(source, target, sems.at[17 + i])
        for i, (source, target) in enumerate(
            ((extras_in, extras), (high_in, high), (low_in, low))
        )
    ]
    for copy in arrivals:
        copy.start()
    take_rows(tiles, emb_ref, 0)
    take_rows(tiles, og, 4)

    tags = tiles[pl.ds(64, FRAMES, stride=CHUNK), :]
    ids = lax.broadcasted_iota(jnp.int32, (FRAMES, ACTIONS), 1).astype(f32)
    pick = jnp.transpose((tags == ids).astype(f32)).astype(bf16)

    emb = emb_ref[...]
    scale = lax.rsqrt(jnp.mean(emb * emb, axis=1, keepdims=True) + 1e-06)
    arrivals[0].wait()
    spacing = extras[:HALF, :]
    gain = jnp.concatenate([extras[HALF + HEADS + i:HALF + HEADS + i + 1, :] for i in range(4)], axis=1)
    normed = emb * gain * scale
    parts = split(normed)
    for copy in arrivals[1:]:
        copy.wait()
    for block in range(QKV // 256):
        cols = slice(block * 256, block * 256 + 256)
        value = dot3(parts, (high[:, cols], low[:, cols]))
        if block < D // 256:
            value = value * 0.125
        qkv_h[:, cols], qkv_l[:, cols] = split(value)
    og_parts = split(og[...])
    gm_h[...], gm_l[...] = split(dot3(og_parts, (high[:, QKV:], low[:, QKV:]), NT))

    lane = lax.broadcasted_iota(jnp.int32, (ROWS, PAIR), 1) < HEAD
    upper = lax.broadcasted_iota(jnp.int32, (ROWS, PAIR), 0) < HALF
    own_half = lane == upper
    first = lane[:HALF]
    zero = jnp.zeros((ROWS, PAIR), bf16)

    def both_heads(parts):
        twice = [jnp.where(own_half, jnp.concatenate([v, v], axis=0), zero) for v in parts]
        return jnp.concatenate([twice[0], twice[1], twice[0]], axis=1)

    def wide(parts):
        return jnp.concatenate([parts[0], parts[0], parts[1]], axis=1)

    def tall(parts):
        return jnp.concatenate([parts[0], parts[0], parts[1]], axis=0)

    def left(value):
        high_part, low_part = split(value)
        return jnp.concatenate([high_part, low_part, high_part], axis=1)

    def turned(value):
        return jnp.concatenate([jnp.transpose(value[:HALF]), jnp.transpose(value[HALF:])], axis=0)

    def pick_lanes(value):
        return jnp.where(first, value[:HALF], value[HALF:])

    for pair in range(HEADS // 2):
        slope = jnp.concatenate(
            [extras[HALF + pair * 2 + i:HALF + pair * 2 + i + 1, :] * spacing for i in range(2)], axis=0
        )
        at = [slice(kind * D + pair * PAIR, kind * D + (pair + 1) * PAIR) for kind in range(3)]
        for g in range(2):
            rows = slice(g * HALF, g * HALF + HALF)
            q, k, v = [(qkv_h[rows, cols], qkv_l[rows, cols]) for cols in at]
            gmp = (gm_h[rows, at[0]], gm_l[rows, at[0]])
            scores = dot(both_heads(q), wide(k), NT) - slope
            raised = jnp.exp(scores - jnp.max(scores, axis=1, keepdims=True))
            weights = raised * (1.0 / jnp.sum(raised, axis=1, keepdims=True))
            d_w = dot(both_heads(gmp), wide(v), NT)
            ds = weights * (d_w - jnp.sum(d_w * weights, axis=1, keepdims=True))
            mixed[rows, at[0]] = pick_lanes(dot(left(weights), tall(v)))
            dq = pick_lanes(dot(left(ds), tall(k))) * 0.125
            dk = pick_lanes(dot(left(turned(ds)), tall(q)))
            dv = pick_lanes(dot(left(turned(weights)), tall(gmp)))
            for cols, value in zip(at, (dq, dk, dv)):
                gr_h[rows, cols], gr_l[rows, cols] = split(value)

    def copy_tiles(tile, count, index):
        part = (slice(None), slice(None), pl.ds(tile, count))
        return pltpu.make_async_copy(grads.at[part], grads_out.at[part], sems.at[index])

    copies = []

    def send_tiles(tile, count, index):
        copies.append(copy_tiles(tile, count, index))
        copies[-1].start()

    def place_columns(block, value):
        for y in YS:
            for side in CS:
                for x in XS:
                    for zh in ZHS:
                        r = y * 128 + zh * 64 + side * 32 + x * 8
                        for half in range(2):
                            grads[y * 2 + side, x, (zh * 8 + block) * 2 + half] = value[
                                r:r + 8, half * 128:half * 128 + 128
                            ]
        for zh in ZHS:
            send_tiles((zh * 8 + block) * 2, 2, block * 2 + zh)

    gn = dot3((gr_h[...], gr_l[...]), (high[:, :QKV], low[:, :QKV]), NT)
    gain_sum = jnp.sum(gn * emb * scale, axis=0, keepdims=True)
    u = gn * gain
    along = jnp.sum(u * emb, axis=1, keepdims=True) * (scale * scale * scale) * (1.0 / D)
    tokens = og[...] + (u * scale - emb * along)
    total = jnp.zeros((FRAMES, D), f32)
    for p in range(OWN):
        piece = tokens[p * FRAMES:(p + 1) * FRAMES, :]
        for k in range(4):
            tokens_new[pl.ds(k * 8 + p, FRAMES, stride=32), :] = piece[:, k * 128:(k + 1) * 128]
        total = total + piece
    copies.append(pltpu.make_async_copy(tokens_new, tokens_out, sems.at[16]))
    copies[-1].start()
    total_h, total_l = split(total)
    table = dot(pick, total_h) + dot(pick, total_l)
    gain_tile = jnp.concatenate(
        [gain_sum[:, i * 64:(i + 1) * 64] for i in range(8)], axis=0
    )
    gain_tile = jnp.concatenate([gain_tile, jnp.zeros((8, 64), f32)], axis=1
    )
    for x in XS:
        for side in CS:
            for k in range(8):
                r, start = x * 32 + (k // 2) * 8, side * 256 + (k % 2) * 128
                tables[side, x, k] = table[r:r + 8, start:start + 128]
            tables[side, x, 8] = gain_tile
    normt = split(jnp.transpose(normed))
    for block in range(QKV // 256):
        cols = slice(block * 256, block * 256 + 256)
        place_columns(block, dot3(normt, (gr_h[:, cols], gr_l[:, cols])))
    mixt = split(jnp.transpose(mixed[...]))
    for block in range(2):
        cols = slice(block * 256, block * 256 + 256)
        place_columns(6 + block, dot3(mixt, (og_parts[0][:, cols], og_parts[1][:, cols])))
    for copy in copies:
        copy.wait()


def call(kernel, outs, scratch, scalars, *arrays, name, far_ins=0, far_outs=0, limit=60, work=None):
    vmem = pl.BlockSpec(memory_space=pltpu.VMEM)
    smem = pl.BlockSpec(memory_space=pltpu.SMEM)
    hbm = pl.BlockSpec(memory_space=pltpu.HBM)
    return pl.pallas_call(
        kernel,
        out_shape=outs,
        in_specs=[smem] * len(scalars) + [vmem] * (len(arrays) - far_ins) + [hbm] * far_ins,
        out_specs=[hbm] * far_outs + [vmem] * (len(outs) - far_outs),
        scratch_shapes=scratch,
        compiler_params=pltpu.CompilerParams(vmem_limit_bytes=limit * 1024 * 1024),
        cost_estimate=work
        and pl.CostEstimate(flops=work, bytes_accessed=0, transcendentals=0),
        name=name,
    )(*scalars, *arrays)


def shape(*dims, kind=f32):
    return jax.ShapeDtypeStruct(dims, kind)


def far_weights(own, quarter):
    row = jnp.stack([quarter] + [lax.ppermute(quarter, "tm", turn_x(i)) for i in range(1, NX)])
    row, own = lax.optimization_barrier((row, own))
    far = jnp.concatenate([row] + [lax.ppermute(row, "dp", turn_y(i)) for i in range(1, NY)])
    return own, far, lax.ppermute(far, "dp", SWAP_CORE)


def shards(
    video_tokens, actions, frame_times, act_table, norm_gain, w_qkv, w_out, slopes, out_grad
):
    t, d = lax.axis_index("tm"), lax.axis_index("dp")
    x, y, zh, c = t // NZL, d // (NZH * NC), (d // NC) % NZH, d % NC
    place = jnp.stack([x, y, zh, c]).astype(jnp.int32)

    payload, mine, quarter = call(
        front_kernel,
        [shape(FRAMES * CHUNK, 128), shape(32, QKV + D), shape(8, QKV + D)],
        [],
        (place, actions.reshape(1)),
        act_table, video_tokens[0, 0], out_grad[0, 0], w_qkv, w_out,
        name="front",
    )
    own = lax.all_gather(mine, "dp", axis_index_groups=YC_GROUPS)
    quarter = lax.ppermute(quarter, "dp", SWAP_ZH)
    quarter = call(
        pass_kernel, [shape(8, QKV + D)], [], (), quarter, name="swapped", work=20000000000
    )[0]
    high, low = call(
        weights_kernel,
        [shape(D, QKV + D, kind=bf16), shape(D, QKV + D, kind=bf16)],
        [],
        (place,),
        *far_weights(own, quarter),
        name="weights",
    )
    tiles = exchange(payload.reshape(FRAMES, CHUNK, 1, 128), "tm")

    times = jnp.tile(frame_times[0].astype(f32), HALF // FRAMES)
    i = lax.broadcasted_iota(jnp.int32, (HALF, HALF), 0)
    j = lax.broadcasted_iota(jnp.int32, (HALF, HALF), 1)
    seen = (i // FRAMES == j // FRAMES) & (j <= i)
    spacing = jnp.where(seen, times[:, None] - times[None, :], f32(1e30))
    extras = jnp.concatenate(
        [
            spacing, jnp.broadcast_to(slopes[:, None], (HEADS, 128)),
            norm_gain.reshape(4, 128), jnp.zeros((4, 128), f32),
        ]
    )

    grads, tokens_back, tables = call(
        sublayer_kernel,
        [
            shape(NY * NC, NX, TILES, 8, 128), shape(ROWS * 4, 128),
            shape(NC, NX, 9, 8, 128),
        ],
        [
            pltpu.VMEM((NY * NC, NX, TILES, 8, 128), f32), pltpu.VMEM((ROWS * 4, 128), f32),
            pltpu.SemaphoreType.DMA((20,)), pltpu.VMEM((HALF + 16, 128), f32),
            pltpu.VMEM((D, QKV + D), bf16), pltpu.VMEM((D, QKV + D), bf16),
            pltpu.VMEM((ROWS, D), f32), pltpu.VMEM((ROWS, D), f32),
            pltpu.VMEM((ROWS, QKV), bf16), pltpu.VMEM((ROWS, QKV), bf16),
            pltpu.VMEM((ROWS, D), bf16), pltpu.VMEM((ROWS, D), bf16),
            pltpu.VMEM((ROWS, D), f32),
            pltpu.VMEM((ROWS, QKV), bf16), pltpu.VMEM((ROWS, QKV), bf16),
        ],
        (),
        tiles.reshape(FRAMES * CHUNK, 128), extras, high, low,
        name="sublayer", far_ins=3, far_outs=2, limit=52,
    )
    tokens_there = exchange(tokens_back.reshape(FRAMES, 4, OWN, 128), "tm")

    row = lax.psum_scatter(
        grads, "dp", scatter_dimension=0, axis_index_groups=YC_GROUPS, tiled=True
    ).reshape(NX, TILES, 8, 128)
    part = lax.dynamic_index_in_dim(tables, c, 0, False) + lax.ppermute(
        lax.dynamic_index_in_dim(tables, 1 - c, 0, False), "dp", SWAP_CORE
    )
    for bit in (1, 2):
        part = part + lax.ppermute(part, "dp", swap_y(bit))
    part, tokens_there = lax.optimization_barrier((part, tokens_there))
    part = jnp.sum(exchange(part, "tm", X_GROUPS), axis=0)
    grad_tokens = call(
        unpack_kernel, [shape(ROWS, D)], [], (), tokens_there, name="unpack"
    )[0]
    row, part, grad_tokens = lax.optimization_barrier((row, part, grad_tokens))
    plane = jnp.sum(exchange(row, "tm", X_GROUPS), axis=0)
    column = jnp.concatenate(
        [
            plane.reshape(16, 16, 1, 128),
            jnp.tile(part[:8], (2, 1, 1)).reshape(16, 8, 1, 128),
            jnp.tile(part[8], (2, 1)).reshape(16, 1, 1, 128),
        ],
        axis=1,
    )
    total = jnp.sum(exchange(column, BOTH, Z_GROUPS), axis=0)

    line = exchange(jnp.broadcast_to(total, (NZL, 25, 1, 128)), "tm", ZL_GROUPS)
    grad_gain = line[:, 24, 0, :64].reshape(D)
    line = line[:, :24].reshape(NZL, 3, 8, 128)
    sheet = exchange(jnp.broadcast_to(line, (NX, NZL, 3, 8, 128)), "tm", X_GROUPS)
    main = sheet[:, :, :2].transpose(0, 3, 1, 2, 4).reshape(32, QKV + D)
    half = sheet[:, :, 2].reshape(NX, 4, 2, 8, 128).transpose(0, 1, 3, 2, 4).reshape(ACTIONS, 256)
    other = lax.ppermute(half, "dp", SWAP_CORE)
    grad_table = jnp.where(
        c == 0, jnp.concatenate([half, other], axis=1), jnp.concatenate([other, half], axis=1)
    )
    return (
        grad_tokens.reshape(1, 1, ROWS, D),
        main[:, :QKV],
        main[:, QKV:],
        grad_table,
        grad_gain,
    )


def solution(mesh):
    return jax.shard_map(
        shards,
        mesh=mesh,
        in_specs=(
            P("dp", "tm", None, None),
            P("dp", "tm"),
            P("dp", None),
            P(),
            P(),
            P("dp", None),
            P("dp", None),
            P(),
            P("dp", "tm", None, None),
        ),
        out_specs=(P("dp", "tm", None, None), P("dp", None), P("dp", None), P(), P()),
        check_vma=False,
    )
```

```python
import functools

import jax
import jax.numpy as jnp
from jax import lax
from jax.experimental import pallas as pl
from jax.experimental.pallas import tpu as pltpu
from jax.sharding import PartitionSpec as P

NX, NZL, NY, NZH, NC = 4, 8, 4, 2, 2
D, QKV, HEADS, HEAD, FRAMES, OWN = 512, 1536, 8, 64, 32, 8
ROWS = FRAMES * OWN
HALF = ROWS // 2
PAIR = 2 * HEAD
ACTIONS = 128
TILES = 32
CHUNK = 65
f32, bf16 = jnp.float32, jnp.bfloat16
BOTH = ("tm", "dp")


def tm_of(x, zl):
    return x * NZL + zl


def dp_of(y, zh, c):
    return (y * NZH + zh) * NC + c


def flat_of(x, zl, y, zh, c):
    return tm_of(x, zl) * (NY * NZH * NC) + dp_of(y, zh, c)


XS, ZLS, YS, ZHS, CS = range(NX), range(NZL), range(NY), range(NZH), range(NC)
X_GROUPS = [[tm_of(x, zl) for x in XS] for zl in ZLS]
ZL_GROUPS = [[tm_of(x, zl) for zl in ZLS] for x in XS]
YC_GROUPS = [[dp_of(y, zh, c) for y in YS for c in CS] for zh in ZHS]
Z_GROUPS = [
    [flat_of(x, zl, y, zh, c) for zh in ZHS for zl in ZLS] for x in XS for y in YS for c in CS
]
SWAP_CORE = [(dp_of(y, zh, c), dp_of(y, zh, 1 - c)) for y in YS for zh in ZHS for c in CS]
SWAP_ZH = [(dp_of(y, zh, c), dp_of(y, 1 - zh, c)) for y in YS for zh in ZHS for c in CS]


def turn_y(step):
    return [(dp_of(y, zh, c), dp_of((y + step) % NY, zh, c)) for y in YS for zh in ZHS for c in CS]


def swap_y(bit):
    return [(dp_of(y, zh, c), dp_of(y ^ bit, zh, c)) for y in YS for zh in ZHS for c in CS]


def turn_x(step):
    return [(tm_of(x, zl), tm_of((x + step) % NX, zl)) for x in XS for zl in ZLS]


def exchange(value, axis, groups=None):
    return lax.all_to_all(value, axis, 0, 0, axis_index_groups=groups, tiled=True)


def split(value):
    high = value.astype(bf16)
    return high, (value - high.astype(f32)).astype(bf16)


NN = (((1,), (0,)), ((), ()))
NT = (((1,), (1,)), ((), ()))


def dot(a, b, dims=NN):
    return lax.dot_general(a, b, dims, preferred_element_type=f32)


def dot3(a, b, dims=NN):
    return dot(a[0], b[0], dims) + (dot(a[0], b[1], dims) + dot(a[1], b[0], dims))


def take_rows(tiles, rows, start):
    for p in range(OWN):
        for k in range(4):
            rows[p * FRAMES:(p + 1) * FRAMES, k * 128:(k + 1) * 128] = tiles[
                pl.ds((start + k) * 8 + p, FRAMES, stride=CHUNK), :
            ]


def pass_kernel(value, out):
    out[...] = value[...]


def front_kernel(place, action, act_table, video, og, w_qkv, w_out, out, mine, quarter):
    mine[:, :QKV] = w_qkv[...]
    mine[:, QKV:] = w_out[...]
    x = pl.multiple_of(place[0] * 8, 8)
    quarter[:, :QKV] = w_qkv[pl.ds(x, 8), :]
    quarter[:, QKV:] = w_out[pl.ds(x, 8), :]
    row = act_table[pl.ds(action[0], 1), :]
    tag = jnp.zeros((1, 128), f32) + action[0].astype(f32)
    for f in range(FRAMES):
        rows = slice(f * OWN, f * OWN + OWN)
        for k in range(D // 128):
            cols = slice(k * 128, k * 128 + 128)
            out[f * CHUNK + k * 8:f * CHUNK + k * 8 + 8, :] = video[rows, cols] + row[:, cols]
            out[f * CHUNK + 32 + k * 8:f * CHUNK + 40 + k * 8, :] = og[rows, cols]
        out[f * CHUNK + 64:f * CHUNK + 65, :] = tag


def unpack_kernel(tiles, out):
    for f in range(FRAMES):
        for k in range(D // 128):
            out[f * OWN:f * OWN + OWN, k * 128:k * 128 + 128] = tiles[f, k]


def weights_kernel(place, own, far_mine, far_other, high, low):
    x, y, zh, c = place[0], place[1], place[2], place[3]
    for y_to in YS:
        for side in CS:
            at = pl.ds(pl.multiple_of(y_to * 128 + zh * 64 + side * 32, 32), 32)
            high[at, :], low[at, :] = split(own[y_to * 2 + side])
        turn_y = lax.rem(y - y_to + NY, NY) * NX
        for x_to in range(0, NX, 2):
            turns = [turn_y + lax.rem(x - x_to - i + NX, NX) for i in range(2)]
            for side, ref in ((c, far_mine), (1 - c, far_other)):
                rows = jnp.concatenate([ref[turn] for turn in turns], axis=0)
                at = y_to * 128 + (1 - zh) * 64 + side * 32 + x_to * 8
                at = pl.ds(pl.multiple_of(at, 16), 16)
                high[at, :], low[at, :] = split(rows)


def sublayer_kernel(
    tiles, extras_in, high_in, low_in,
    grads_out, tokens_out, tables,
    grads, tokens_new, sems, extras, high, low, emb_ref, og, qkv_h, qkv_l, gm_h, gm_l, mixed, gr_h, gr_l,
):
    extras_copy = pltpu.make_async_copy(extras_in, extras, sems.at[17])
    extras_copy.start()
    arrivals = []
    for chunk in range(4):
        cols = pl.ds(chunk * 512, 512)
        arrivals.append([
            pltpu.make_async_copy(source.at[:, cols], target.at[:, cols], sems.at[18 + chunk * 2 + i])
            for i, (source, target) in enumerate(((high_in, high), (low_in, low)))
        ])
        for copy in arrivals[-1]:
            copy.start()
    take_rows(tiles, emb_ref, 0)
    take_rows(tiles, og, 4)

    tags = tiles[pl.ds(64, FRAMES, stride=CHUNK), :]
    ids = lax.broadcasted_iota(jnp.int32, (FRAMES, ACTIONS), 1).astype(f32)
    pick = jnp.transpose((tags == ids).astype(f32)).astype(bf16)

    emb = emb_ref[...]
    scale = lax.rsqrt(jnp.mean(emb * emb, axis=1, keepdims=True) + 1e-06)
    extras_copy.wait()
    spacing = extras[:HALF, :]
    gain = jnp.concatenate([extras[HALF + HEADS + i:HALF + HEADS + i + 1, :] for i in range(4)], axis=1)
    normed = emb * gain * scale
    parts = split(normed)
    for block in range(QKV // 256):
        if block % 2 == 0:
            for copy in arrivals[block // 2]:
                copy.wait()
        cols = slice(block * 256, block * 256 + 256)
        value = dot3(parts, (high[:, cols], low[:, cols]))
        if block < D // 256:
            value = value * 0.125
        qkv_h[:, cols], qkv_l[:, cols] = split(value)
    og_parts = split(og[...])
    for copy in arrivals[3]:
        copy.wait()
    gm_h[...], gm_l[...] = split(dot3(og_parts, (high[:, QKV:], low[:, QKV:]), NT))

    lane = lax.broadcasted_iota(jnp.int32, (ROWS, PAIR), 1) < HEAD
    upper = lax.broadcasted_iota(jnp.int32, (ROWS, PAIR), 0) < HALF
    own_half = lane == upper
    first = lane[:HALF]
    zero = jnp.zeros((ROWS, PAIR), bf16)

    def both_heads(parts):
        twice = [jnp.where(own_half, jnp.concatenate([v, v], axis=0), zero) for v in parts]
        return jnp.concatenate([twice[0], twice[1], twice[0]], axis=1)

    def wide(parts):
        return jnp.concatenate([parts[0], parts[0], parts[1]], axis=1)

    def tall(parts):
        return jnp.concatenate([parts[0], parts[0], parts[1]], axis=0)

    def left(value):
        high_part, low_part = split(value)
        return jnp.concatenate([high_part, low_part, high_part], axis=1)

    def turned(value):
        return jnp.concatenate([jnp.transpose(value[:HALF]), jnp.transpose(value[HALF:])], axis=0)

    def pick_lanes(value):
        return jnp.where(first, value[:HALF], value[HALF:])

    for pair in range(HEADS // 2):
        slope = jnp.concatenate(
            [extras[HALF + pair * 2 + i:HALF + pair * 2 + i + 1, :] * spacing for i in range(2)], axis=0
        )
        at = [slice(kind * D + pair * PAIR, kind * D + (pair + 1) * PAIR) for kind in range(3)]
        for g in range(2):
            rows = slice(g * HALF, g * HALF + HALF)
            q, k, v = [(qkv_h[rows, cols], qkv_l[rows, cols]) for cols in at]
            gmp = (gm_h[rows, at[0]], gm_l[rows, at[0]])
            scores = dot(both_heads(q), wide(k), NT) - slope
            raised = jnp.exp(scores - jnp.max(scores, axis=1, keepdims=True))
            weights = raised * (1.0 / jnp.sum(raised, axis=1, keepdims=True))
            d_w = dot(both_heads(gmp), wide(v), NT)
            ds = weights * (d_w - jnp.sum(d_w * weights, axis=1, keepdims=True))
            mixed[rows, at[0]] = pick_lanes(dot(left(weights), tall(v)))
            dq = pick_lanes(dot(left(ds), tall(k))) * 0.125
            dk = pick_lanes(dot(left(turned(ds)), tall(q)))
            dv = pick_lanes(dot(left(turned(weights)), tall(gmp)))
            for cols, value in zip(at, (dq, dk, dv)):
                gr_h[rows, cols], gr_l[rows, cols] = split(value)

    def copy_tiles(tile, count, index):
        part = (slice(None), slice(None), pl.ds(tile, count))
        return pltpu.make_async_copy(grads.at[part], grads_out.at[part], sems.at[index])

    copies = []

    def send_tiles(tile, count, index):
        copies.append(copy_tiles(tile, count, index))
        copies[-1].start()

    def place_columns(block, value):
        for y in YS:
            for side in CS:
                for x in XS:
                    for zh in ZHS:
                        r = y * 128 + zh * 64 + side * 32 + x * 8
                        for half in range(2):
                            grads[y * 2 + side, x, (zh * 8 + block) * 2 + half] = value[
                                r:r + 8, half * 128:half * 128 + 128
                            ]
        for zh in ZHS:
            send_tiles((zh * 8 + block) * 2, 2, block * 2 + zh)

    gn = dot3((gr_h[...], gr_l[...]), (high[:, :QKV], low[:, :QKV]), NT)
    gain_sum = jnp.sum(gn * emb * scale, axis=0, keepdims=True)
    u = gn * gain
    along = jnp.sum(u * emb, axis=1, keepdims=True) * (scale * scale * scale) * (1.0 / D)
    tokens = og[...] + (u * scale - emb * along)
    total = jnp.zeros((FRAMES, D), f32)
    for p in range(OWN):
        piece = tokens[p * FRAMES:(p + 1) * FRAMES, :]
        for k in range(4):
            tokens_new[pl.ds(k * 8 + p, FRAMES, stride=32), :] = piece[:, k * 128:(k + 1) * 128]
        total = total + piece
    copies.append(pltpu.make_async_copy(tokens_new, tokens_out, sems.at[16]))
    copies[-1].start()
    total_h, total_l = split(total)
    table = dot(pick, total_h) + dot(pick, total_l)
    gain_tile = jnp.concatenate(
        [gain_sum[:, i * 64:(i + 1) * 64] for i in range(8)], axis=0
    )
    gain_tile = jnp.concatenate([gain_tile, jnp.zeros((8, 64), f32)], axis=1
    )
    for x in XS:
        for side in CS:
            for k in range(8):
                r, start = x * 32 + (k // 2) * 8, side * 256 + (k % 2) * 128
                tables[side, x, k] = table[r:r + 8, start:start + 128]
            tables[side, x, 8] = gain_tile
    normt = split(jnp.transpose(normed))
    for block in range(QKV // 256):
        cols = slice(block * 256, block * 256 + 256)
        place_columns(block, dot3(normt, (gr_h[:, cols], gr_l[:, cols])))
    mixt = split(jnp.transpose(mixed[...]))
    for block in range(2):
        cols = slice(block * 256, block * 256 + 256)
        place_columns(6 + block, dot3(mixt, (og_parts[0][:, cols], og_parts[1][:, cols])))
    for copy in copies:
        copy.wait()


def call(kernel, outs, scratch, scalars, *arrays, name, far_ins=0, far_outs=0, limit=60, work=None):
    vmem = pl.BlockSpec(memory_space=pltpu.VMEM)
    smem = pl.BlockSpec(memory_space=pltpu.SMEM)
    hbm = pl.BlockSpec(memory_space=pltpu.HBM)
    return pl.pallas_call(
        kernel,
        out_shape=outs,
        in_specs=[smem] * len(scalars) + [vmem] * (len(arrays) - far_ins) + [hbm] * far_ins,
        out_specs=[hbm] * far_outs + [vmem] * (len(outs) - far_outs),
        scratch_shapes=scratch,
        compiler_params=pltpu.CompilerParams(vmem_limit_bytes=limit * 1024 * 1024),
        cost_estimate=work
        and pl.CostEstimate(flops=work, bytes_accessed=0, transcendentals=0),
        name=name,
    )(*scalars, *arrays)


def shape(*dims, kind=f32):
    return jax.ShapeDtypeStruct(dims, kind)


def far_weights(own, quarter):
    row = jnp.stack([quarter] + [lax.ppermute(quarter, "tm", turn_x(i)) for i in range(1, NX)])
    row, own = lax.optimization_barrier((row, own))
    far = jnp.concatenate([row] + [lax.ppermute(row, "dp", turn_y(i)) for i in range(1, NY)])
    return own, far, lax.ppermute(far, "dp", SWAP_CORE)


def shards(
    video_tokens, actions, frame_times, act_table, norm_gain, w_qkv, w_out, slopes, out_grad
):
    t, d = lax.axis_index("tm"), lax.axis_index("dp")
    x, y, zh, c = t // NZL, d // (NZH * NC), (d // NC) % NZH, d % NC
    place = jnp.stack([x, y, zh, c]).astype(jnp.int32)

    payload, mine, quarter = call(
        front_kernel,
        [shape(FRAMES * CHUNK, 128), shape(32, QKV + D), shape(8, QKV + D)],
        [],
        (place, actions.reshape(1)),
        act_table, video_tokens[0, 0], out_grad[0, 0], w_qkv, w_out,
        name="front",
    )
    own = lax.all_gather(mine, "dp", axis_index_groups=YC_GROUPS)
    quarter = lax.ppermute(quarter, "dp", SWAP_ZH)
    quarter = call(
        pass_kernel, [shape(8, QKV + D)], [], (), quarter, name="swapped", work=20000000000
    )[0]
    high, low = call(
        weights_kernel,
        [shape(D, QKV + D, kind=bf16), shape(D, QKV + D, kind=bf16)],
        [],
        (place,),
        *far_weights(own, quarter),
        name="weights",
    )
    tiles = exchange(payload.reshape(FRAMES, CHUNK, 1, 128), "tm")

    times = jnp.tile(frame_times[0].astype(f32), HALF // FRAMES)
    i = lax.broadcasted_iota(jnp.int32, (HALF, HALF), 0)
    j = lax.broadcasted_iota(jnp.int32, (HALF, HALF), 1)
    seen = (i // FRAMES == j // FRAMES) & (j <= i)
    spacing = jnp.where(seen, times[:, None] - times[None, :], f32(1e30))
    extras = jnp.concatenate(
        [
            spacing, jnp.broadcast_to(slopes[:, None], (HEADS, 128)),
            norm_gain.reshape(4, 128), jnp.zeros((4, 128), f32),
        ]
    )

    grads, tokens_back, tables = call(
        sublayer_kernel,
        [
            shape(NY * NC, NX, TILES, 8, 128), shape(ROWS * 4, 128),
            shape(NC, NX, 9, 8, 128),
        ],
        [
            pltpu.VMEM((NY * NC, NX, TILES, 8, 128), f32), pltpu.VMEM((ROWS * 4, 128), f32),
            pltpu.SemaphoreType.DMA((26,)), pltpu.VMEM((HALF + 16, 128), f32),
            pltpu.VMEM((D, QKV + D), bf16), pltpu.VMEM((D, QKV + D), bf16),
            pltpu.VMEM((ROWS, D), f32), pltpu.VMEM((ROWS, D), f32),
            pltpu.VMEM((ROWS, QKV), bf16), pltpu.VMEM((ROWS, QKV), bf16),
            pltpu.VMEM((ROWS, D), bf16), pltpu.VMEM((ROWS, D), bf16),
            pltpu.VMEM((ROWS, D), f32),
            pltpu.VMEM((ROWS, QKV), bf16), pltpu.VMEM((ROWS, QKV), bf16),
        ],
        (),
        tiles.reshape(FRAMES * CHUNK, 128), extras, high, low,
        name="sublayer", far_ins=3, far_outs=2, limit=52,
    )
    tokens_there = exchange(tokens_back.reshape(FRAMES, 4, OWN, 128), "tm")

    row = lax.psum_scatter(
        grads, "dp", scatter_dimension=0, axis_index_groups=YC_GROUPS, tiled=True
    ).reshape(NX, TILES, 8, 128)
    part = lax.dynamic_index_in_dim(tables, c, 0, False) + lax.ppermute(
        lax.dynamic_index_in_dim(tables, 1 - c, 0, False), "dp", SWAP_CORE
    )
    for bit in (1, 2):
        part = part + lax.ppermute(part, "dp", swap_y(bit))
    part, tokens_there = lax.optimization_barrier((part, tokens_there))
    part = jnp.sum(exchange(part, "tm", X_GROUPS), axis=0)
    grad_tokens = call(
        unpack_kernel, [shape(ROWS, D)], [], (), tokens_there, name="unpack"
    )[0]
    row, part, grad_tokens = lax.optimization_barrier((row, part, grad_tokens))
    plane = jnp.sum(exchange(row, "tm", X_GROUPS), axis=0)
    column = jnp.concatenate(
        [
            plane.reshape(16, 16, 1, 128),
            jnp.tile(part[:8], (2, 1, 1)).reshape(16, 8, 1, 128),
            jnp.tile(part[8], (2, 1)).reshape(16, 1, 1, 128),
        ],
        axis=1,
    )
    total = jnp.sum(exchange(column, BOTH, Z_GROUPS), axis=0)

    line = exchange(jnp.broadcast_to(total, (NZL, 25, 1, 128)), "tm", ZL_GROUPS)
    grad_gain = line[:, 24, 0, :64].reshape(D)
    line = line[:, :24].reshape(NZL, 3, 8, 128)
    sheet = exchange(jnp.broadcast_to(line, (NX, NZL, 3, 8, 128)), "tm", X_GROUPS)
    main = sheet[:, :, :2].transpose(0, 3, 1, 2, 4).reshape(32, QKV + D)
    half = sheet[:, :, 2].reshape(NX, 4, 2, 8, 128).transpose(0, 1, 3, 2, 4).reshape(ACTIONS, 256)
    other = lax.ppermute(half, "dp", SWAP_CORE)
    grad_table = jnp.where(
        c == 0, jnp.concatenate([half, other], axis=1), jnp.concatenate([other, half], axis=1)
    )
    return (
        grad_tokens.reshape(1, 1, ROWS, D),
        main[:, :QKV],
        main[:, QKV:],
        grad_table,
        grad_gain,
    )


def solution(mesh):
    return jax.shard_map(
        shards,
        mesh=mesh,
        in_specs=(
            P("dp", "tm", None, None),
            P("dp", "tm"),
            P("dp", None),
            P(),
            P(),
            P("dp", None),
            P("dp", None),
            P(),
            P("dp", "tm", None, None),
        ),
        out_specs=(P("dp", "tm", None, None), P("dp", None), P("dp", None), P(), P()),
        check_vma=False,
    )
```

```python
import functools

import jax
import jax.numpy as jnp
from jax import lax
from jax.experimental import pallas as pl
from jax.experimental.pallas import tpu as pltpu
from jax.sharding import PartitionSpec as P

NX, NZL, NY, NZH, NC = 4, 8, 4, 2, 2
D, QKV, HEADS, HEAD, FRAMES, OWN = 512, 1536, 8, 64, 32, 8
ROWS = FRAMES * OWN
HALF = ROWS // 2
PAIR = 2 * HEAD
ACTIONS = 128
TILES = 32
CHUNK = 65
f32, bf16 = jnp.float32, jnp.bfloat16
BOTH = ("tm", "dp")


def tm_of(x, zl):
    return x * NZL + zl


def dp_of(y, zh, c):
    return (y * NZH + zh) * NC + c


def flat_of(x, zl, y, zh, c):
    return tm_of(x, zl) * (NY * NZH * NC) + dp_of(y, zh, c)


XS, ZLS, YS, ZHS, CS = range(NX), range(NZL), range(NY), range(NZH), range(NC)
X_GROUPS = [[tm_of(x, zl) for x in XS] for zl in ZLS]
ZL_GROUPS = [[tm_of(x, zl) for zl in ZLS] for x in XS]
YC_GROUPS = [[dp_of(y, zh, c) for y in YS for c in CS] for zh in ZHS]
Z_GROUPS = [
    [flat_of(x, zl, y, zh, c) for zh in ZHS for zl in ZLS] for x in XS for y in YS for c in CS
]
SWAP_CORE = [(dp_of(y, zh, c), dp_of(y, zh, 1 - c)) for y in YS for zh in ZHS for c in CS]
SWAP_ZH = [(dp_of(y, zh, c), dp_of(y, 1 - zh, c)) for y in YS for zh in ZHS for c in CS]


def turn_y(step):
    return [(dp_of(y, zh, c), dp_of((y + step) % NY, zh, c)) for y in YS for zh in ZHS for c in CS]


def swap_y(bit):
    return [(dp_of(y, zh, c), dp_of(y ^ bit, zh, c)) for y in YS for zh in ZHS for c in CS]


def turn_x(step):
    return [(tm_of(x, zl), tm_of((x + step) % NX, zl)) for x in XS for zl in ZLS]


def exchange(value, axis, groups=None):
    return lax.all_to_all(value, axis, 0, 0, axis_index_groups=groups, tiled=True)


def split(value):
    high = value.astype(bf16)
    return high, (value - high.astype(f32)).astype(bf16)


NN = (((1,), (0,)), ((), ()))
NT = (((1,), (1,)), ((), ()))


def dot(a, b, dims=NN):
    return lax.dot_general(a, b, dims, preferred_element_type=f32)


def dot3(a, b, dims=NN):
    return dot(a[0], b[0], dims) + (dot(a[0], b[1], dims) + dot(a[1], b[0], dims))


def take_rows(tiles, rows, start):
    for p in range(OWN):
        for k in range(4):
            rows[p * FRAMES:(p + 1) * FRAMES, k * 128:(k + 1) * 128] = tiles[
                pl.ds((start + k) * 8 + p, FRAMES, stride=CHUNK), :
            ]


def pass_kernel(value, out):
    out[...] = value[...]


def front_kernel(place, action, act_table, video, og, w_qkv, w_out, out, mine, quarter):
    mine[:, :QKV] = w_qkv[...]
    mine[:, QKV:] = w_out[...]
    x = pl.multiple_of(place[0] * 8, 8)
    quarter[:, :QKV] = w_qkv[pl.ds(x, 8), :]
    quarter[:, QKV:] = w_out[pl.ds(x, 8), :]
    row = act_table[pl.ds(action[0], 1), :]
    tag = jnp.zeros((1, 128), f32) + action[0].astype(f32)
    for f in range(FRAMES):
        rows = slice(f * OWN, f * OWN + OWN)
        for k in range(D // 128):
            cols = slice(k * 128, k * 128 + 128)
            out[f * CHUNK + k * 8:f * CHUNK + k * 8 + 8, :] = video[rows, cols] + row[:, cols]
            out[f * CHUNK + 32 + k * 8:f * CHUNK + 40 + k * 8, :] = og[rows, cols]
        out[f * CHUNK + 64:f * CHUNK + 65, :] = tag


def unpack_kernel(tiles, out):
    for f in range(FRAMES):
        for k in range(D // 128):
            out[f * OWN:f * OWN + OWN, k * 128:k * 128 + 128] = tiles[f, k]


def weights_kernel(place, own, far_mine, far_other, high, low):
    x, y, zh, c = place[0], place[1], place[2], place[3]
    for y_to in YS:
        for side in CS:
            at = pl.ds(pl.multiple_of(y_to * 128 + zh * 64 + side * 32, 32), 32)
            high[at, :], low[at, :] = split(own[y_to * 2 + side])
        turn_y = lax.rem(y - y_to + NY, NY) * NX
        for x_to in range(0, NX, 2):
            turns = [turn_y + lax.rem(x - x_to - i + NX, NX) for i in range(2)]
            for side, ref in ((c, far_mine), (1 - c, far_other)):
                rows = jnp.concatenate([ref[turn] for turn in turns], axis=0)
                at = y_to * 128 + (1 - zh) * 64 + side * 32 + x_to * 8
                at = pl.ds(pl.multiple_of(at, 16), 16)
                high[at, :], low[at, :] = split(rows)


def sublayer_kernel(
    tiles, extras_in, high_in, low_in,
    grads_out, tokens_out, tables,
    grads, tokens_new, sems, extras, high, low, emb_ref, og, qkv_h, qkv_l, gm_h, gm_l, mixed, gr_h, gr_l,
):
    arrivals = [
        pltpu.make_async_copy(source, target, sems.at[17 + i])
        for i, (source, target) in enumerate(
            ((extras_in, extras), (high_in, high), (low_in, low))
        )
    ]
    for copy in arrivals:
        copy.start()
    take_rows(tiles, emb_ref, 0)
    take_rows(tiles, og, 4)

    tags = tiles[pl.ds(64, FRAMES, stride=CHUNK), :]
    ids = lax.broadcasted_iota(jnp.int32, (FRAMES, ACTIONS), 1).astype(f32)
    pick = jnp.transpose((tags == ids).astype(f32)).astype(bf16)

    emb = emb_ref[...]
    scale = lax.rsqrt(jnp.mean(emb * emb, axis=1, keepdims=True) + 1e-06)
    arrivals[0].wait()
    spacing = extras[:HALF, :]
    gain = jnp.concatenate([extras[HALF + HEADS + i:HALF + HEADS + i + 1, :] for i in range(4)], axis=1)
    normed = emb * gain * scale
    parts = split(normed)
    for copy in arrivals[1:]:
        copy.wait()
    for block in range(QKV // 256):
        cols = slice(block * 256, block * 256 + 256)
        value = dot3(parts, (high[:, cols], low[:, cols]))
        if block < D // 256:
            value = value * 0.125
        qkv_h[:, cols], qkv_l[:, cols] = split(value)
    og_parts = split(og[...])
    gm_h[...], gm_l[...] = split(dot3(og_parts, (high[:, QKV:], low[:, QKV:]), NT))

    lane = lax.broadcasted_iota(jnp.int32, (ROWS, PAIR), 1) < HEAD
    upper = lax.broadcasted_iota(jnp.int32, (ROWS, PAIR), 0) < HALF
    own_half = lane == upper
    first = lane[:HALF]
    zero = jnp.zeros((ROWS, PAIR), bf16)

    def both_heads(parts):
        twice = [jnp.where(own_half, jnp.concatenate([v, v], axis=0), zero) for v in parts]
        return jnp.concatenate([twice[0], twice[1], twice[0]], axis=1)

    def wide(parts):
        return jnp.concatenate([parts[0], parts[0], parts[1]], axis=1)

    def tall(parts):
        return jnp.concatenate([parts[0], parts[0], parts[1]], axis=0)

    def left(value):
        high_part, low_part = split(value)
        return jnp.concatenate([high_part, low_part, high_part], axis=1)

    def turned(value):
        return jnp.concatenate([jnp.transpose(value[:HALF]), jnp.transpose(value[HALF:])], axis=0)

    def pick_lanes(value):
        return jnp.where(first, value[:HALF], value[HALF:])

    for pair in range(HEADS // 2):
        slope = jnp.concatenate(
            [extras[HALF + pair * 2 + i:HALF + pair * 2 + i + 1, :] * spacing for i in range(2)], axis=0
        )
        at = [slice(kind * D + pair * PAIR, kind * D + (pair + 1) * PAIR) for kind in range(3)]
        for g in range(2):
            rows = slice(g * HALF, g * HALF + HALF)
            q, k, v = [(qkv_h[rows, cols], qkv_l[rows, cols]) for cols in at]
            gmp = (gm_h[rows, at[0]], gm_l[rows, at[0]])
            scores = dot(both_heads(q), wide(k), NT) - slope
            raised = jnp.exp(scores - jnp.max(scores, axis=1, keepdims=True))
            weights = raised * (1.0 / jnp.sum(raised, axis=1, keepdims=True))
            d_w = dot(both_heads(gmp), wide(v), NT)
            ds = weights * (d_w - jnp.sum(d_w * weights, axis=1, keepdims=True))
            mixed[rows, at[0]] = pick_lanes(dot(left(weights), tall(v)))
            dq = pick_lanes(dot(left(ds), tall(k))) * 0.125
            dk = pick_lanes(dot(left(turned(ds)), tall(q)))
            dv = pick_lanes(dot(left(turned(weights)), tall(gmp)))
            for cols, value in zip(at, (dq, dk, dv)):
                gr_h[rows, cols], gr_l[rows, cols] = split(value)

    def copy_tiles(tile, count, index):
        part = (slice(None), slice(None), pl.ds(tile, count))
        return pltpu.make_async_copy(grads.at[part], grads_out.at[part], sems.at[index])

    copies = []

    def send_tiles(tile, count, index):
        copies.append(copy_tiles(tile, count, index))
        copies[-1].start()

    def place_columns(block, value):
        for y in YS:
            for side in CS:
                for x in XS:
                    for zh in ZHS:
                        r = y * 128 + zh * 64 + side * 32 + x * 8
                        for half in range(2):
                            grads[y * 2 + side, x, (zh * 8 + block) * 2 + half] = value[
                                r:r + 8, half * 128:half * 128 + 128
                            ]
        for zh in ZHS:
            send_tiles((zh * 8 + block) * 2, 2, block * 2 + zh)

    gn = dot3((gr_h[...], gr_l[...]), (high[:, :QKV], low[:, :QKV]), NT)
    gain_sum = jnp.sum(gn * emb * scale, axis=0, keepdims=True)
    u = gn * gain
    along = jnp.sum(u * emb, axis=1, keepdims=True) * (scale * scale * scale) * (1.0 / D)
    tokens = og[...] + (u * scale - emb * along)
    total = jnp.zeros((FRAMES, D), f32)
    for p in range(OWN):
        piece = tokens[p * FRAMES:(p + 1) * FRAMES, :]
        for k in range(4):
            tokens_new[pl.ds(k * 8 + p, FRAMES, stride=32), :] = piece[:, k * 128:(k + 1) * 128]
        total = total + piece
    copies.append(pltpu.make_async_copy(tokens_new, tokens_out, sems.at[16]))
    copies[-1].start()
    total_h, total_l = split(total)
    table = dot(pick, total_h) + dot(pick, total_l)
    gain_tile = jnp.concatenate(
        [gain_sum[:, i * 64:(i + 1) * 64] for i in range(8)], axis=0
    )
    gain_tile = jnp.concatenate([gain_tile, jnp.zeros((8, 64), f32)], axis=1
    )
    for x in XS:
        for side in CS:
            for k in range(8):
                r, start = x * 32 + (k // 2) * 8, side * 256 + (k % 2) * 128
                tables[side, x, k] = table[r:r + 8, start:start + 128]
            tables[side, x, 8] = gain_tile
    normt = split(jnp.transpose(normed))
    for block in range(QKV // 256):
        cols = slice(block * 256, block * 256 + 256)
        place_columns(block, dot3(normt, (gr_h[:, cols], gr_l[:, cols])))
    mixt = split(jnp.transpose(mixed[...]))
    for block in range(2):
        cols = slice(block * 256, block * 256 + 256)
        place_columns(6 + block, dot3(mixt, (og_parts[0][:, cols], og_parts[1][:, cols])))
    for copy in copies:
        copy.wait()


def call(kernel, outs, scratch, scalars, *arrays, name, far_ins=0, far_outs=0, limit=60, work=None):
    vmem = pl.BlockSpec(memory_space=pltpu.VMEM)
    smem = pl.BlockSpec(memory_space=pltpu.SMEM)
    hbm = pl.BlockSpec(memory_space=pltpu.HBM)
    return pl.pallas_call(
        kernel,
        out_shape=outs,
        in_specs=[smem] * len(scalars) + [vmem] * (len(arrays) - far_ins) + [hbm] * far_ins,
        out_specs=[hbm] * far_outs + [vmem] * (len(outs) - far_outs),
        scratch_shapes=scratch,
        compiler_params=pltpu.CompilerParams(vmem_limit_bytes=limit * 1024 * 1024),
        cost_estimate=work
        and pl.CostEstimate(flops=work, bytes_accessed=0, transcendentals=0),
        name=name,
    )(*scalars, *arrays)


def shape(*dims, kind=f32):
    return jax.ShapeDtypeStruct(dims, kind)


def far_weights(own, quarter):
    row = jnp.stack([quarter] + [lax.ppermute(quarter, "tm", turn_x(i)) for i in range(1, NX)])
    row, own = lax.optimization_barrier((row, own))
    far = jnp.concatenate([row] + [lax.ppermute(row, "dp", turn_y(i)) for i in range(1, NY)])
    return own, far, lax.ppermute(far, "dp", SWAP_CORE)


def shards(
    video_tokens, actions, frame_times, act_table, norm_gain, w_qkv, w_out, slopes, out_grad
):
    t, d = lax.axis_index("tm"), lax.axis_index("dp")
    x, y, zh, c = t // NZL, d // (NZH * NC), (d // NC) % NZH, d % NC
    place = jnp.stack([x, y, zh, c]).astype(jnp.int32)

    payload, mine, quarter = call(
        front_kernel,
        [shape(FRAMES * CHUNK, 128), shape(32, QKV + D), shape(8, QKV + D)],
        [],
        (place, actions.reshape(1)),
        act_table, video_tokens[0, 0], out_grad[0, 0], w_qkv, w_out,
        name="front",
    )
    own = lax.all_gather(mine, "dp", axis_index_groups=YC_GROUPS)
    quarter = lax.ppermute(quarter, "dp", SWAP_ZH)
    quarter = call(
        pass_kernel, [shape(8, QKV + D)], [], (), quarter, name="swapped", work=20000000000
    )[0]
    high, low = call(
        weights_kernel,
        [shape(D, QKV + D, kind=bf16), shape(D, QKV + D, kind=bf16)],
        [],
        (place,),
        *far_weights(own, quarter),
        name="weights",
    )
    tiles = exchange(payload.reshape(FRAMES, CHUNK, 1, 128), "tm")

    times = jnp.tile(frame_times[0].astype(f32), HALF // FRAMES)
    i = lax.broadcasted_iota(jnp.int32, (HALF, HALF), 0)
    j = lax.broadcasted_iota(jnp.int32, (HALF, HALF), 1)
    seen = (i // FRAMES == j // FRAMES) & (j <= i)
    spacing = jnp.where(seen, times[:, None] - times[None, :], f32(1e30))
    extras = jnp.concatenate(
        [
            spacing, jnp.broadcast_to(slopes[:, None], (HEADS, 128)),
            norm_gain.reshape(4, 128), jnp.zeros((4, 128), f32),
        ]
    )

    grads, tokens_back, tables = call(
        sublayer_kernel,
        [
            shape(NY * NC, NX, TILES, 8, 128), shape(ROWS * 4, 128),
            shape(NC, NX, 9, 8, 128),
        ],
        [
            pltpu.VMEM((NY * NC, NX, TILES, 8, 128), f32), pltpu.VMEM((ROWS * 4, 128), f32),
            pltpu.SemaphoreType.DMA((20,)), pltpu.VMEM((HALF + 16, 128), f32),
            pltpu.VMEM((D, QKV + D), bf16), pltpu.VMEM((D, QKV + D), bf16),
            pltpu.VMEM((ROWS, D), f32), pltpu.VMEM((ROWS, D), f32),
            pltpu.VMEM((ROWS, QKV), bf16), pltpu.VMEM((ROWS, QKV), bf16),
            pltpu.VMEM((ROWS, D), bf16), pltpu.VMEM((ROWS, D), bf16),
            pltpu.VMEM((ROWS, D), f32),
            pltpu.VMEM((ROWS, QKV), bf16), pltpu.VMEM((ROWS, QKV), bf16),
        ],
        (),
        tiles.reshape(FRAMES * CHUNK, 128), extras, high, low,
        name="sublayer", far_ins=3, far_outs=2, limit=52,
    )
    tokens_there = exchange(tokens_back.reshape(FRAMES, 4, OWN, 128), "tm")

    row = lax.psum_scatter(
        grads, "dp", scatter_dimension=0, axis_index_groups=YC_GROUPS, tiled=True
    ).reshape(NX, TILES, 8, 128)
    part = lax.dynamic_index_in_dim(tables, c, 0, False) + lax.ppermute(
        lax.dynamic_index_in_dim(tables, 1 - c, 0, False), "dp", SWAP_CORE
    )
    for bit in (2, 1):
        part = part + lax.ppermute(part, "dp", swap_y(bit))
    part, tokens_there = lax.optimization_barrier((part, tokens_there))
    part = jnp.sum(exchange(part, "tm", X_GROUPS), axis=0)
    grad_tokens = call(
        unpack_kernel, [shape(ROWS, D)], [], (), tokens_there, name="unpack"
    )[0]
    row, part, grad_tokens = lax.optimization_barrier((row, part, grad_tokens))
    plane = jnp.sum(exchange(row, "tm", X_GROUPS), axis=0)
    column = jnp.concatenate(
        [
            plane.reshape(16, 16, 1, 128),
            jnp.tile(part[:8], (2, 1, 1)).reshape(16, 8, 1, 128),
            jnp.tile(part[8], (2, 1)).reshape(16, 1, 1, 128),
        ],
        axis=1,
    )
    total = jnp.sum(exchange(column, BOTH, Z_GROUPS), axis=0)

    line = exchange(jnp.broadcast_to(total, (NZL, 25, 1, 128)), "tm", ZL_GROUPS)
    grad_gain = line[:, 24, 0, :64].reshape(D)
    line = line[:, :24].reshape(NZL, 3, 8, 128)
    sheet = exchange(jnp.broadcast_to(line, (NX, NZL, 3, 8, 128)), "tm", X_GROUPS)
    main = sheet[:, :, :2].transpose(0, 3, 1, 2, 4).reshape(32, QKV + D)
    half = sheet[:, :, 2].reshape(NX, 4, 2, 8, 128).transpose(0, 1, 3, 2, 4).reshape(ACTIONS, 256)
    other = lax.ppermute(half, "dp", SWAP_CORE)
    grad_table = jnp.where(
        c == 0, jnp.concatenate([half, other], axis=1), jnp.concatenate([other, half], axis=1)
    )
    return (
        grad_tokens.reshape(1, 1, ROWS, D),
        main[:, :QKV],
        main[:, QKV:],
        grad_table,
        grad_gain,
    )


def solution(mesh):
    return jax.shard_map(
        shards,
        mesh=mesh,
        in_specs=(
            P("dp", "tm", None, None),
            P("dp", "tm"),
            P("dp", None),
            P(),
            P(),
            P("dp", None),
            P("dp", None),
            P(),
            P("dp", "tm", None, None),
        ),
        out_specs=(P("dp", "tm", None, None), P("dp", None), P("dp", None), P(), P()),
        check_vma=False,
    )
```
